512 devices in a mesh: tm: 128 (over x, z, y_hi, core), panel: 4 (over y_lo).
Axes of the slice: x: 4, y: 8 (y_hi: 2, y_lo: 4; y = y_hi * 4 + y_lo), z: 8, core: 2. Of those that a mesh axis runs over, the one named last changes fastest.
Arguments:
- forward_props: bfloat16 [2, 128, 1024, 1024], P(None, 'tm', 'panel'), may hold values from -2 to 2
Outputs:
- prefix_props: bfloat16 [2, 128, 1024, 1024], P(None, 'tm', 'panel')
The draws below stay inside these ranges and needn't reach their ends.
All inputs are finite; a program needn't handle non-finite values.
Results may differ from the reference program's by a relative error of at most 0.0057.
Values may be sent and summed in bfloat16 or wider, within the bound.
A program may use at most 64 MiB of HBM per device.

```python
import math
import jax
import jax.numpy as jnp
from jax import lax

M = 1024
SECTIONS = 2
SLICES = 128


def assemble_props(phase_key, magnitude_key, noise, lowest):
    phases = jax.random.uniform(phase_key, (SLICES, M), jnp.float32, -math.pi, math.pi)
    magnitude = jax.random.uniform(magnitude_key, (SLICES, M), jnp.float32, lowest, 1.0)
    identity = (jnp.arange(M)[:, None] == jnp.arange(M)[None, :]).astype(jnp.float32)
    real_part = identity[None] * (magnitude * jnp.cos(phases))[:, None, :] + noise[0]
    imag_part = identity[None] * (magnitude * jnp.sin(phases))[:, None, :] + noise[1]
    return jnp.stack([real_part, imag_part]).astype(jnp.bfloat16)


def draw_forward_props(key, part):
    key = jax.random.fold_in(key, 11)
    noise_key, phase_key, magnitude_key = jax.random.split(key, 3)
    noise = jax.random.normal(noise_key, (2, SLICES, M, M), jnp.float32) * (0.5 / math.sqrt(M))
    lowest = 0.6
    return assemble_props(phase_key, magnitude_key, noise, lowest)


def setup_inputs(seed: int = 0) -> dict:
    key_of = jax.random.split(jax.random.key(seed), 2)
    return {
        "forward_props": draw_forward_props(jax.random.fold_in(key_of[1], 71), 0),
    }


def complex_product(left, right):
    high = lax.Precision.HIGHEST
    left_re = left[0].astype(jnp.float32)
    left_im = left[1].astype(jnp.float32)
    right_re = right[0].astype(jnp.float32)
    right_im = right[1].astype(jnp.float32)
    real_part = jnp.dot(left_re, right_re, precision=high) - jnp.dot(left_im, right_im, precision=high)
    imag_part = jnp.dot(left_re, right_im, precision=high) + jnp.dot(left_im, right_re, precision=high)
    return jnp.stack([real_part, imag_part]).astype(jnp.bfloat16)


def doubling_level(chain, distance):
    count = chain.shape[0]
    partner = jnp.concatenate([jnp.zeros_like(chain[:distance]), chain[:count - distance]], axis=0)
    product = lax.map(lambda pair: complex_product(pair[0], pair[1]), (chain, partner))
    position = jnp.arange(count, dtype=jnp.int32)
    return jnp.where((position >= distance)[:, None, None, None], product, chain)


def reference(forward_props):
    chain = jnp.moveaxis(forward_props, 1, 0)
    for level in range(SECTIONS):
        chain = doubling_level(chain, 2 ** level)
    return jnp.moveaxis(chain, 0, 1)
```

```python
import functools

import jax
import jax.numpy as jnp
from jax import lax
from jax.experimental import pallas as pl
from jax.experimental.pallas import tpu as pltpu
from jax.sharding import PartitionSpec as P

PANELS = 4
CHUNKS = 8
BANDS = 4

bf16, f32 = jnp.bfloat16, jnp.float32


def dot(a, b):
    return jnp.dot(a, b, preferred_element_type=f32)


def when(cond):
    return pl.when(cond)


def loop(n, body):
    def step(i, carry):
        body(i)
        return carry

    lax.fori_loop(0, n, step, 0)


def kernel(
    tm_size, x_ref, out_ref, own, obuf, o2buf, ebuf, dsend, drecv, dloc, gbuf, acc,
    in_sem, o_recv, o_right, o_left, o_z, o2_recv, e_recv, e_right, e_left, e_in, d_recv, d_out, d_in,
):
    rows, width = x_ref.shape[1], x_ref.shape[2]
    cols = width // CHUNKS
    band = rows // BANDS
    tm, p = lax.axis_index("tm"), lax.axis_index("panel")
    core = lax.rem(tm, 2)
    site = tm // 2

    def at(shift, panel):
        return (lax.rem(tm + shift + tm_size, tm_size), panel)

    def remote(src, dst, send, recv, where):
        return pltpu.make_async_remote_copy(
            src_ref=src, dst_ref=dst, send_sem=send, recv_sem=recv,
            device_id=where, device_id_type=pl.DeviceIdType.MESH,
        )

    def o_rows(q, c):
        return pl.ds(pl.multiple_of(q * rows + c * band, band), band)

    def o_copy(q, c, sems, where, dst=None, recv=None):
        piece = obuf.at[:, o_rows(q, c), :]
        target = piece if dst is None else dst.at[:, o_rows(q, c), :]
        arrive = (o_recv if recv is None else recv).at[q, c]
        return remote(piece, target, sems.at[q, c], arrive, where)

    def o_r(q, c):
        return o_copy(q, c, o_right, at(0, lax.rem(p + 1, PANELS)))

    def o_l(q, c):
        return o_copy(q, c, o_left, at(0, lax.rem(p + PANELS - 1, PANELS)))

    def o_up(q, c):
        return o_copy(q, c, o_z, at(3, p), o2buf, o2_recv)

    def e_piece(q, j):
        return ebuf.at[j, :, pl.ds(pl.multiple_of(q * rows, rows), rows), :]

    def e_copy(q, j, sems, panel):
        return remote(e_piece(q, j), e_piece(q, j), sems.at[q, j], e_recv.at[q, j], at(0, panel))

    def e_r(q, j):
        return e_copy(q, j, e_right, lax.rem(p + 1, PANELS))

    def e_l(q, j):
        return e_copy(q, j, e_left, lax.rem(p + PANELS - 1, PANELS))

    def e_over(j):
        columns = pl.ds(pl.multiple_of(j * cols, cols), cols)
        return remote(own.at[:, :, columns], e_piece(p, j), e_in.at[j], e_recv.at[p, j], at(1, p))

    def d_next(j):
        return remote(dsend.at[j], drecv.at[j], d_out.at[j], d_recv.at[j], at(1, PANELS - 1 - p))

    def d_pass(j, panel):
        return remote(drecv.at[j], drecv.at[j], d_out.at[j], d_recv.at[j], at(0, panel))

    def d_over(j):
        return remote(drecv.at[j], drecv.at[j], d_in.at[j], d_recv.at[j], at(1, p))

    edge = (p == 0) | (p == PANELS - 1)
    low = p < PANELS // 2

    def arrival(i):
        inner = jnp.where(i < 4, jnp.where(lax.rem(i, 2) == 0, i // 2, 7 - i // 2), i - 2)
        a = jnp.where(edge, i, inner)
        j = jnp.where(low, a, CHUNKS - 1 - a)
        return a, j

    load = pltpu.make_async_copy(x_ref, own, in_sem)
    load.start()

    barrier = pltpu.get_barrier_semaphore()

    def greet(where):
        pl.semaphore_signal(barrier, inc=1, device_id=where, device_id_type=pl.DeviceIdType.MESH)

    @when(p > 0)
    def _():
        greet(at(0, p - 1))

    @when(p < PANELS - 1)
    def _():
        greet(at(0, p + 1))

    @when(core == 0)
    def _():
        greet(at(1, p))
        greet(at(-3, p))

        @when(edge)
        def _():
            greet(at(-1, PANELS - 1 - p))

    @when(core == 1)
    def _():
        greet(at(-1, p))
        greet(at(3, p))

        @when(edge)
        def _():
            greet(at(1, PANELS - 1 - p))

    load.wait()
    pl.semaphore_wait(barrier, 4)

    @when(core == 0)
    def _():
        loop(CHUNKS, lambda j: e_over(j).start())
        acc[...] = jnp.zeros_like(acc)

        def gather_o2(i):
            q, c = i // BANDS, lax.rem(i, BANDS)
            o_copy(q, c, o_z, at(-3, p), o2buf, o2_recv).wait_recv()

        loop(PANELS * BANDS, gather_o2)

        def step(i):
            a, j = arrival(i)
            d_over(j).wait_recv()

            @when((p == 0) & (a < 6))
            def _():
                d_pass(j, 1).start()

            @when((p == 3) & (a < 6))
            def _():
                d_pass(j, 2).start()

            @when((p == 1) & (a < 2))
            def _():
                d_pass(j, 2).start()

            @when((p == 2) & (a < 2))
            def _():
                d_pass(j, 1).start()

            d_over(j).start()
            columns = pl.ds(pl.multiple_of(j * cols, cols), cols)
            er, ei = own[0], own[1]
            dr, di = drecv[j, 0], drecv[j, 1]
            gr = (dot(er, dr) - dot(ei, di)).astype(bf16)
            gi = (dot(er, di) + dot(ei, dr)).astype(bf16)
            gbuf[0, :, columns] = gr
            gbuf[1, :, columns] = gi
            tr, ti = o2buf[0, columns, :], o2buf[1, columns, :]
            acc[0] += dot(gr, tr) - dot(gi, ti)
            acc[1] += dot(gr, ti) + dot(gi, tr)

        loop(CHUNKS, step)
        out_ref[...] = jnp.where(site == 0, own[...], jnp.where(site == 1, gbuf[...], acc[...].astype(bf16)))

        def drain(i):
            a, j = arrival(i)
            e_over(i).wait_send()
            d_over(j).wait_send()

            @when(a < jnp.where(edge, 6, 2))
            def _():
                d_pass(j, 1).wait_send()

        loop(CHUNKS, drain)

    @when(core == 1)
    def _():
        obuf[:, pl.ds(pl.multiple_of(p * rows, rows), rows), :] = own[...]

        def pass_o(q, c, right, left):
            @when(right & (p < PANELS - 1))
            def _():
                o_r(q, c).start()

            @when(left & (p > 0))
            def _():
                o_l(q, c).start()

            o_up(q, c).start()

        loop(BANDS, lambda c: pass_o(p, c, True, True))

        def hop(n):
            def one(c):
                @when(p - 1 - n >= 0)
                def _():
                    o_r(p - 1 - n, c).wait_recv()
                    pass_o(p - 1 - n, c, True, False)

                @when(p + 1 + n < PANELS)
                def _():
                    o_l(p + 1 + n, c).wait_recv()
                    pass_o(p + 1 + n, c, False, True)

            loop(BANDS, one)

        def own_e():
            loop(CHUNKS, lambda j: e_over(j).wait_recv())

        hop(0)
        own_e()

        @when(p == 0)
        def _():
            loop(CHUNKS, lambda j: e_r(0, j).start())

        @when(p == 3)
        def _():
            loop(CHUNKS, lambda j: e_l(3, CHUNKS - 1 - j).start())

        hop(1)

        @when(p == 1)
        def _():
            def one(j):
                e_r(1, j).start()
                e_r(0, j).wait_recv()
                e_r(0, j).start()

            loop(CHUNKS, one)

        @when(p == 2)
        def _():
            def one(i):
                j = CHUNKS - 1 - i
                e_l(2, j).start()
                e_l(3, j).wait_recv()
                e_l(3, j).start()

            loop(CHUNKS, one)

        hop(2)

        @when(p == 1)
        def _():
            loop((PANELS - 1) * BANDS, lambda i: o_l(1 + i // BANDS, lax.rem(i, BANDS)).wait_send())

            def one(i):
                j = CHUNKS - 1 - i
                e_l(1, j).start()
                e_l(2, j).wait_recv()
                e_l(2, j).start()
                e_l(3, j).wait_recv()
                e_l(3, j).start()

            loop(CHUNKS, one)
            loop(CHUNKS, lambda j: e_r(0, j).wait_send())

        @when(p == 2)
        def _():
            loop((PANELS - 1) * BANDS, lambda i: o_r(i // BANDS, lax.rem(i, BANDS)).wait_send())

            def one(j):
                e_r(2, j).start()
                e_r(1, j).wait_recv()
                e_r(1, j).start()
                e_r(0, j).wait_recv()
                e_r(0, j).start()

            loop(CHUNKS, one)
            loop(CHUNKS, lambda j: e_l(3, j).wait_send())

        def product(q, j):
            here = pl.ds(pl.multiple_of(q * rows, rows), rows)
            ar, ai = obuf[0, here, :], obuf[1, here, :]
            br, bi = ebuf[j, 0], ebuf[j, 1]
            re = (dot(ar, br) - dot(ai, bi)).astype(bf16)
            im = (dot(ar, bi) + dot(ai, br)).astype(bf16)
            return re, im

        @when(edge)
        def _():
            def one(i):
                j = jnp.where(p == 0, CHUNKS - 1 - i, i)

                @when(p == 0)
                def _():
                    loop(PANELS - 1, lambda q: e_l(q + 1, j).wait_recv())

                @when(p == 3)
                def _():
                    loop(PANELS - 1, lambda q: e_r(q, j).wait_recv())

                def block(q):
                    here = pl.ds(pl.multiple_of(q * rows, rows), rows)
                    re, im = product(q, j)
                    dsend[j, 0, here, :] = re
                    dsend[j, 1, here, :] = im

                loop(PANELS, block)
                d_next(j).start()
                mine = pl.ds(pl.multiple_of(p * rows, rows), rows)
                columns = pl.ds(pl.multiple_of(j * cols, cols), cols)
                dloc[:, :, columns] = dsend[j, :, mine, :]

            loop(CHUNKS, one)

        @when(p == 1)
        def _():
            loop(CHUNKS, lambda j: e_l(2, j).wait_send())

        @when(~edge)
        def _():
            def one(j):
                columns = pl.ds(pl.multiple_of(j * cols, cols), cols)
                re, im = product(p, j)
                dloc[0, :, columns] = re
                dloc[1, :, columns] = im

            loop(CHUNKS, one)

        def step(i):
            _, j = arrival(i)
            d_over(j).wait_recv()
            columns = pl.ds(pl.multiple_of(j * cols, cols), cols)
            ar, ai = dloc[0], dloc[1]
            br, bi = drecv[j, 0], drecv[j, 1]
            re = (dot(ar, br) - dot(ai, bi)).astype(bf16)
            im = (dot(ar, bi) + dot(ai, br)).astype(bf16)
            out_ref[0, :, columns] = jnp.where(site == 0, dloc[0, :, columns], re)
            out_ref[1, :, columns] = jnp.where(site == 0, dloc[1, :, columns], im)

        loop(CHUNKS, step)

        def drain_o(i):
            q, c = i // BANDS, lax.rem(i, BANDS)
            o_up(q, c).wait_send()

            @when((q <= p) & (p < PANELS - 1) & (p != 2))
            def _():
                o_r(q, c).wait_send()

            @when((q >= p) & (p > 0) & (p != 1))
            def _():
                o_l(q, c).wait_send()

        loop(PANELS * BANDS, drain_o)

        def drain_e(j):
            @when(p == 0)
            def _():
                e_r(0, j).wait_send()

            @when(p == 3)
            def _():
                e_l(3, j).wait_send()

            @when(p == 1)
            def _():
                e_r(1, j).wait_send()
                e_l(1, j).wait_send()
                e_l(3, j).wait_send()

            @when(p == 2)
            def _():
                e_l(2, j).wait_send()
                loop(PANELS - 1, lambda q: e_r(q, j).wait_send())

            @when(edge)
            def _():
                d_next(j).wait_send()

        loop(CHUNKS, drain_e)


def shards(forward_props):
    x = forward_props[:, 0]
    _, rows, width = x.shape
    cols = width // CHUNKS
    dma = pltpu.SemaphoreType.DMA
    tm_size = lax.axis_size("tm")
    out = pl.pallas_call(
        functools.partial(kernel, tm_size),
        out_shape=jax.ShapeDtypeStruct(x.shape, bf16),
        in_specs=[pl.BlockSpec(memory_space=pl.ANY)],
        out_specs=pl.BlockSpec(memory_space=pltpu.VMEM),
        scratch_shapes=[
            pltpu.VMEM(x.shape, bf16),
            pltpu.VMEM((2, width, width), bf16),
            pltpu.VMEM((2, width, width), bf16),
            pltpu.VMEM((CHUNKS, 2, width, cols), bf16),
            pltpu.VMEM((CHUNKS, 2, width, cols), bf16),
            pltpu.VMEM((CHUNKS, 2, width, cols), bf16),
            pltpu.VMEM(x.shape, bf16),
            pltpu.VMEM(x.shape, bf16),
            pltpu.VMEM(x.shape, f32),
            dma,
            dma((PANELS, BANDS)),
            dma((PANELS, BANDS)),
            dma((PANELS, BANDS)),
            dma((PANELS, BANDS)),
            dma((PANELS, BANDS)),
            dma((PANELS, CHUNKS)),
            dma((PANELS, CHUNKS)),
            dma((PANELS, CHUNKS)),
            dma((CHUNKS,)),
            dma((CHUNKS,)),
            dma((CHUNKS,)),
            dma((CHUNKS,)),
        ],
        compiler_params=pltpu.CompilerParams(
            collective_id=0, has_side_effects=True, vmem_limit_bytes=48 * 2**20
        ),
        name="prefix_products",
    )(x)
    return out[:, None]


def solution(mesh):
    placed = (P(None, "tm", "panel", None),)
    return jax.shard_map(
        shards, mesh=mesh, in_specs=placed, out_specs=P(None, "tm", "panel", None), check_vma=False
    )
```

```python
import functools

import jax
import jax.numpy as jnp
from jax import lax
from jax.experimental import pallas as pl
from jax.experimental.pallas import tpu as pltpu
from jax.sharding import PartitionSpec as P

PANELS = 4
CHUNKS = 8
WINDOW = 2
BANDS = 4

bf16, f32 = jnp.bfloat16, jnp.float32


def dot(a, b):
    return jnp.dot(a, b, preferred_element_type=f32)


def when(cond):
    return pl.when(cond)


def loop(n, body):
    def step(i, carry):
        body(i)
        return carry

    lax.fori_loop(0, n, step, 0)


def kernel(
    tm_size, x_ref, out_ref, own, obuf, o2buf, ebuf, dsend, drecv, dloc, gbuf, acc,
    in_sem, o_recv, o_right, o_left, o_z, o2_recv, e_recv, e_right, e_left, e_in, d_recv, d_out, d_in,
):
    rows, width = x_ref.shape[1], x_ref.shape[2]
    cols = width // CHUNKS
    band = rows // BANDS
    tm, p = lax.axis_index("tm"), lax.axis_index("panel")
    core = lax.rem(tm, 2)
    site = tm // 2

    def at(shift, panel):
        return (lax.rem(tm + shift + tm_size, tm_size), panel)

    def remote(src, dst, send, recv, where):
        return pltpu.make_async_remote_copy(
            src_ref=src, dst_ref=dst, send_sem=send, recv_sem=recv,
            device_id=where, device_id_type=pl.DeviceIdType.MESH,
        )

    def o_rows(q, c):
        return pl.ds(pl.multiple_of(q * rows + c * band, band), band)

    def o_copy(q, c, sems, where, dst=None, recv=None):
        piece = obuf.at[:, o_rows(q, c), :]
        target = piece if dst is None else dst.at[:, o_rows(q, c), :]
        arrive = (o_recv if recv is None else recv).at[q, c]
        return remote(piece, target, sems.at[q, c], arrive, where)

    def o_r(q, c):
        return o_copy(q, c, o_right, at(0, lax.rem(p + 1, PANELS)))

    def o_l(q, c):
        return o_copy(q, c, o_left, at(0, lax.rem(p + PANELS - 1, PANELS)))

    def o_up(q, c):
        return o_copy(q, c, o_z, at(3, p), o2buf, o2_recv)

    def e_piece(q, j):
        return ebuf.at[j, :, pl.ds(pl.multiple_of(q * rows, rows), rows), :]

    def e_copy(q, j, sems, panel):
        return remote(e_piece(q, j), e_piece(q, j), sems.at[q, j], e_recv.at[q, j], at(0, panel))

    def e_r(q, j):
        return e_copy(q, j, e_right, lax.rem(p + 1, PANELS))

    def e_l(q, j):
        return e_copy(q, j, e_left, lax.rem(p + PANELS - 1, PANELS))

    def e_over(j):
        columns = pl.ds(pl.multiple_of(j * cols, cols), cols)
        return remote(own.at[:, :, columns], e_piece(p, j), e_in.at[j], e_recv.at[p, j], at(1, p))

    def d_next(j):
        return remote(dsend.at[j], drecv.at[j], d_out.at[j], d_recv.at[j], at(1, PANELS - 1 - p))

    def d_pass(j, panel):
        return remote(drecv.at[j], drecv.at[j], d_out.at[j], d_recv.at[j], at(0, panel))

    def d_over(j):
        return remote(drecv.at[j], drecv.at[j], d_in.at[j], d_recv.at[j], at(1, p))

    edge = (p == 0) | (p == PANELS - 1)
    low = p < PANELS // 2

    def arrival(i):
        inner = jnp.where(i < 2, i, jnp.where(i == 2, 7, jnp.where(i == 3, 2, jnp.where(i == 4, 6, i - 2))))
        outer = jnp.where(i < 6, i, 13 - i)
        a = jnp.where(edge, outer, inner)
        j = jnp.where(low, a, CHUNKS - 1 - a)
        return a, j

    def passes(a):
        return jnp.where(edge, a < 6, (a < 2) | (a == 7))

    def pass_to(a):
        onward = jnp.where(edge, jnp.where(low, 1, 2), jnp.where(low, 2, 1))
        back = jnp.where(low, 0, PANELS - 1)
        return jnp.where(~edge & (a == 7), back, onward)

    load = pltpu.make_async_copy(x_ref, own, in_sem)
    load.start()

    barrier = pltpu.get_barrier_semaphore()

    def greet(where):
        pl.semaphore_signal(barrier, inc=1, device_id=where, device_id_type=pl.DeviceIdType.MESH)

    @when(p > 0)
    def _():
        greet(at(0, p - 1))

    @when(p < PANELS - 1)
    def _():
        greet(at(0, p + 1))

    @when(core == 0)
    def _():
        greet(at(-3, p))

        @when(edge)
        def _():
            greet(at(-1, PANELS - 1 - p))

    @when(core == 1)
    def _():
        greet(at(-1, p))

    load.wait()
    pl.semaphore_wait(barrier, jnp.where((core == 0) & edge, 2, 3))

    @when(core == 0)
    def _():
        loop(CHUNKS, lambda j: e_over(j).start())
        acc[...] = jnp.zeros_like(acc)

        def take(i):
            a, j = arrival(i)
            d_over(j).wait_recv()

            @when(passes(a))
            def _():
                d_pass(j, pass_to(a)).start()

            d_over(j).start()
            columns = pl.ds(pl.multiple_of(j * cols, cols), cols)
            er, ei = own[0], own[1]
            dr, di = drecv[j, 0], drecv[j, 1]
            gbuf[0, :, columns] = (dot(er, dr) - dot(ei, di)).astype(bf16)
            gbuf[1, :, columns] = (dot(er, di) + dot(ei, dr)).astype(bf16)

        def add(i):
            _, j = arrival(i)

            def rows_in(n):
                o_copy(j // 2, 2 * lax.rem(j, 2) + n, o_z, at(-3, p), o2buf, o2_recv).wait_recv()

            loop(BANDS // 2, rows_in)
            columns = pl.ds(pl.multiple_of(j * cols, cols), cols)
            gr, gi = gbuf[0, :, columns], gbuf[1, :, columns]
            tr, ti = o2buf[0, columns, :], o2buf[1, columns, :]
            acc[0] += dot(gr, tr) - dot(gi, ti)
            acc[1] += dot(gr, ti) + dot(gi, tr)

        def added(i):
            return jnp.where(i < 3, 0, jnp.where(i < 6, 2 * i - 5, i))

        def step(i):
            take(i)

            def more(n, carry):
                add(n)
                return carry

            lax.fori_loop(added(i - 1), added(i), more, 0)

        loop(CHUNKS, step)
        add(CHUNKS - 1)
        out_ref[...] = jnp.where(site == 0, own[...], jnp.where(site == 1, gbuf[...], acc[...].astype(bf16)))

        def drain(i):
            a, j = arrival(i)
            e_over(i).wait_send()
            d_over(j).wait_send()

            @when(passes(a))
            def _():
                d_pass(j, 1).wait_send()

        loop(CHUNKS, drain)

    @when(core == 1)
    def _():
        obuf[:, pl.ds(pl.multiple_of(p * rows, rows), rows), :] = own[...]

        def pass_o(q, c, right, left):
            @when(right & (p < PANELS - 1))
            def _():
                o_r(q, c).start()

            @when(left & (p > 0))
            def _():
                o_l(q, c).start()

            o_up(q, c).start()

        loop(BANDS, lambda c: pass_o(p, c, True, True))

        def hop(n):
            def one(c):
                @when(p - 1 - n >= 0)
                def _():
                    o_r(p - 1 - n, c).wait_recv()
                    pass_o(p - 1 - n, c, True, False)

                @when(p + 1 + n < PANELS)
                def _():
                    o_l(p + 1 + n, c).wait_recv()
                    pass_o(p + 1 + n, c, False, True)

            loop(BANDS, one)

        def own_e():
            loop(CHUNKS, lambda j: e_over(j).wait_recv())

        hop(0)
        own_e()

        @when(p == 0)
        def _():
            loop(CHUNKS, lambda j: e_r(0, j).start())

        @when(p == 3)
        def _():
            loop(CHUNKS, lambda j: e_l(3, CHUNKS - 1 - j).start())

        hop(1)

        @when(p == 1)
        def _():
            def one(j):
                e_r(1, j).start()
                e_r(0, j).wait_recv()
                e_r(0, j).start()

            loop(CHUNKS, one)

        @when(p == 2)
        def _():
            def one(i):
                j = CHUNKS - 1 - i
                e_l(2, j).start()
                e_l(3, j).wait_recv()
                e_l(3, j).start()

            loop(CHUNKS, one)

        hop(2)

        @when(p == 1)
        def _():
            loop((PANELS - 1) * BANDS, lambda i: o_l(1 + i // BANDS, lax.rem(i, BANDS)).wait_send())

            def one(i):
                j = CHUNKS - 1 - i

                @when(i >= WINDOW)
                def _():
                    loop(PANELS - 1, lambda q: e_l(q + 1, j + WINDOW).wait_send())

                e_l(1, j).start()
                e_l(2, j).wait_recv()
                e_l(2, j).start()
                e_l(3, j).wait_recv()
                e_l(3, j).start()

            loop(CHUNKS, one)

        @when(p == 2)
        def _():
            loop((PANELS - 1) * BANDS, lambda i: o_r(i // BANDS, lax.rem(i, BANDS)).wait_send())

            def one(j):
                @when(j >= WINDOW)
                def _():
                    loop(PANELS - 1, lambda q: e_r(q, j - WINDOW).wait_send())

                e_r(2, j).start()
                e_r(1, j).wait_recv()
                e_r(1, j).start()
                e_r(0, j).wait_recv()
                e_r(0, j).start()

            loop(CHUNKS, one)

        def product(q, j):
            here = pl.ds(pl.multiple_of(q * rows, rows), rows)
            ar, ai = obuf[0, here, :], obuf[1, here, :]
            br, bi = ebuf[j, 0], ebuf[j, 1]
            re = (dot(ar, br) - dot(ai, bi)).astype(bf16)
            im = (dot(ar, bi) + dot(ai, br)).astype(bf16)
            return re, im

        @when(edge)
        def _():
            def one(i):
                j = jnp.where(p == 0, CHUNKS - 1 - i, i)

                @when(p == 0)
                def _():
                    loop(PANELS - 1, lambda q: e_l(q + 1, j).wait_recv())

                @when(p == 3)
                def _():
                    loop(PANELS - 1, lambda q: e_r(q, j).wait_recv())

                def block(q):
                    here = pl.ds(pl.multiple_of(q * rows, rows), rows)
                    re, im = product(q, j)
                    dsend[j, 0, here, :] = re
                    dsend[j, 1, here, :] = im

                loop(PANELS, block)

                @when(i < CHUNKS - 1)
                def _():
                    d_next(j).start()

                mine = pl.ds(pl.multiple_of(p * rows, rows), rows)
                columns = pl.ds(pl.multiple_of(j * cols, cols), cols)
                dloc[:, :, columns] = dsend[j, :, mine, :]

            loop(CHUNKS, one)

        @when(~edge)
        def _():
            def one(j):
                columns = pl.ds(pl.multiple_of(j * cols, cols), cols)
                re, im = product(p, j)
                dloc[0, :, columns] = re
                dloc[1, :, columns] = im

            loop(CHUNKS, one)

        def step(i):
            _, j = arrival(i)
            d_over(j).wait_recv()
            columns = pl.ds(pl.multiple_of(j * cols, cols), cols)
            ar, ai = dloc[0], dloc[1]
            br, bi = drecv[j, 0], drecv[j, 1]
            re = (dot(ar, br) - dot(ai, bi)).astype(bf16)
            im = (dot(ar, bi) + dot(ai, br)).astype(bf16)
            out_ref[0, :, columns] = jnp.where(site == 0, dloc[0, :, columns], re)
            out_ref[1, :, columns] = jnp.where(site == 0, dloc[1, :, columns], im)

        loop(CHUNKS, step)

        def drain_o(i):
            q, c = i // BANDS, lax.rem(i, BANDS)
            o_up(q, c).wait_send()

            @when((q <= p) & (p < PANELS - 1) & (p != 2))
            def _():
                o_r(q, c).wait_send()

            @when((q >= p) & (p > 0) & (p != 1))
            def _():
                o_l(q, c).wait_send()

        loop(PANELS * BANDS, drain_o)

        def drain_e(j):
            @when(p == 0)
            def _():
                e_r(0, j).wait_send()

            @when(p == 3)
            def _():
                e_l(3, j).wait_send()

            @when(p == 1)
            def _():
                e_r(0, j).wait_send()
                e_r(1, j).wait_send()

                @when(j < WINDOW)
                def _():
                    loop(PANELS - 1, lambda q: e_l(q + 1, j).wait_send())

            @when(p == 2)
            def _():
                e_l(2, j).wait_send()
                e_l(3, j).wait_send()

                @when(j >= CHUNKS - WINDOW)
                def _():
                    loop(PANELS - 1, lambda q: e_r(q, j).wait_send())

            @when((p == 0) & (j > 0) | (p == PANELS - 1) & (j < CHUNKS - 1))
            def _():
                d_next(j).wait_send()

        loop(CHUNKS, drain_e)


def shards(forward_props):
    x = forward_props[:, 0]
    _, rows, width = x.shape
    cols = width // CHUNKS
    dma = pltpu.SemaphoreType.DMA
    tm_size = lax.axis_size("tm")
    out = pl.pallas_call(
        functools.partial(kernel, tm_size),
        out_shape=jax.ShapeDtypeStruct(x.shape, bf16),
        in_specs=[pl.BlockSpec(memory_space=pl.ANY)],
        out_specs=pl.BlockSpec(memory_space=pltpu.VMEM),
        scratch_shapes=[
            pltpu.VMEM(x.shape, bf16),
            pltpu.VMEM((2, width, width), bf16),
            pltpu.VMEM((2, width, width), bf16),
            pltpu.VMEM((CHUNKS, 2, width, cols), bf16),
            pltpu.VMEM((CHUNKS, 2, width, cols), bf16),
            pltpu.VMEM((CHUNKS, 2, width, cols), bf16),
            pltpu.VMEM(x.shape, bf16),
            pltpu.VMEM(x.shape, bf16),
            pltpu.VMEM(x.shape, f32),
            dma,
            dma((PANELS, BANDS)),
            dma((PANELS, BANDS)),
            dma((PANELS, BANDS)),
            dma((PANELS, BANDS)),
            dma((PANELS, BANDS)),
            dma((PANELS, CHUNKS)),
            dma((PANELS, CHUNKS)),
            dma((PANELS, CHUNKS)),
            dma((CHUNKS,)),
            dma((CHUNKS,)),
            dma((CHUNKS,)),
            dma((CHUNKS,)),
        ],
        compiler_params=pltpu.CompilerParams(
            collective_id=0, has_side_effects=True, vmem_limit_bytes=48 * 2**20
        ),
        name="prefix_products",
    )(x)
    return out[:, None]


def solution(mesh):
    placed = (P(None, "tm", "panel", None),)
    return jax.shard_map(
        shards, mesh=mesh, in_specs=placed, out_specs=P(None, "tm", "panel", None), check_vma=False
    )
```

```python
import functools

import jax
import jax.numpy as jnp
from jax import lax
from jax.experimental import pallas as pl
from jax.experimental.pallas import tpu as pltpu
from jax.sharding import PartitionSpec as P

PANELS = 4
CHUNKS = 8
BANDS = 4

bf16, f32 = jnp.bfloat16, jnp.float32


def dot(a, b):
    return jnp.dot(a, b, preferred_element_type=f32)


def when(cond):
    return pl.when(cond)


def loop(n, body):
    def step(i, carry):
        body(i)
        return carry

    lax.fori_loop(0, n, step, 0)


def kernel(
    tm_size, x_ref, out_ref, own, obuf, o2buf, ebuf, dsend, drecv, dloc, gbuf, acc,
    in_sem, o_recv, o_right, o_left, o_z, o2_recv, e_recv, e_right, e_left, e_in, d_recv, d_out, d_in,
):
    rows, width = x_ref.shape[1], x_ref.shape[2]
    cols = width // CHUNKS
    band = rows // BANDS
    tm, p = lax.axis_index("tm"), lax.axis_index("panel")
    core = lax.rem(tm, 2)
    site, sites = tm // 2, tm_size // 2

    def at(shift, panel):
        return (lax.rem(tm + shift + tm_size, tm_size), panel)

    def remote(src, dst, send, recv, where):
        return pltpu.make_async_remote_copy(
            src_ref=src, dst_ref=dst, send_sem=send, recv_sem=recv,
            device_id=where, device_id_type=pl.DeviceIdType.MESH,
        )

    def o_rows(q, c):
        return pl.ds(pl.multiple_of(q * rows + c * band, band), band)

    def o_copy(q, c, sems, where, dst=None, recv=None):
        piece = obuf.at[:, o_rows(q, c), :]
        target = piece if dst is None else dst.at[:, o_rows(q, c), :]
        arrive = (o_recv if recv is None else recv).at[q, c]
        return remote(piece, target, sems.at[q, c], arrive, where)

    def o_r(q, c):
        return o_copy(q, c, o_right, at(0, lax.rem(p + 1, PANELS)))

    def o_l(q, c):
        return o_copy(q, c, o_left, at(0, lax.rem(p + PANELS - 1, PANELS)))

    def o_up(q, c):
        return o_copy(q, c, o_z, at(3, p), o2buf, o2_recv)

    def e_piece(q, j):
        return ebuf.at[j, :, pl.ds(pl.multiple_of(q * rows, rows), rows), :]

    def e_copy(q, j, sems, panel):
        return remote(e_piece(q, j), e_piece(q, j), sems.at[q, j], e_recv.at[q, j], at(0, panel))

    def e_r(q, j):
        return e_copy(q, j, e_right, lax.rem(p + 1, PANELS))

    def e_l(q, j):
        return e_copy(q, j, e_left, lax.rem(p + PANELS - 1, PANELS))

    def e_over(j):
        columns = pl.ds(pl.multiple_of(j * cols, cols), cols)
        return remote(own.at[:, :, columns], e_piece(p, j), e_in.at[j], e_recv.at[p, j], at(1, p))

    def d_next(j):
        return remote(dsend.at[j], drecv.at[j], d_out.at[j], d_recv.at[j], at(1, PANELS - 1 - p))

    def d_pass(j, panel):
        return remote(drecv.at[j], drecv.at[j], d_out.at[j], d_recv.at[j], at(0, panel))

    def d_over(j):
        return remote(drecv.at[j], drecv.at[j], d_in.at[j], d_recv.at[j], at(1, p))

    odd = lax.rem(site, 2) == 1
    direct_out = jnp.where(odd, 6, 7)
    direct_in = jnp.where(odd, 7, 6)
    edge = (p == 0) | (p == PANELS - 1)
    low = p < PANELS // 2

    def pick(i, values):
        found = values[-1]
        for n in range(len(values) - 1):
            found = jnp.where(i == n, values[n], found)
        return found

    def arrival(i):
        inner = pick(i, (0, 1, 7, 2, 6, 3, 5, 4))
        outer = jnp.where(odd, pick(i, (0, 1, 2, 3, 4, 7, 5, 6)), pick(i, (0, 1, 2, 3, 4, 7, 6, 5)))
        a = jnp.where(edge, outer, inner)
        j = jnp.where(low, a, CHUNKS - 1 - a)
        return a, j

    def passes(a):
        return jnp.where(edge, a < 5, (a < 3) | (a >= direct_in))

    def pass_to(a):
        onward = jnp.where(edge, jnp.where(low, 1, 2), jnp.where(low, 2, 1))
        back = jnp.where(low, 0, PANELS - 1)
        return jnp.where(~edge & (a >= direct_in), back, onward)

    load_e = pltpu.make_async_copy(x_ref, own, in_sem)
    load_o = pltpu.make_async_copy(x_ref, obuf.at[:, pl.ds(pl.multiple_of(p * rows, rows), rows), :], in_sem)
    when(core == 0)(load_e.start)
    when(core == 1)(load_o.start)

    barrier = pltpu.get_barrier_semaphore()

    def greet(where):
        pl.semaphore_signal(barrier, inc=1, device_id=where, device_id_type=pl.DeviceIdType.MESH)

    @when(p > 0)
    def _():
        greet(at(0, p - 1))

    @when(p < PANELS - 1)
    def _():
        greet(at(0, p + 1))

    @when(core == 0)
    def _():
        greet(at(-3, p))

        @when(edge)
        def _():
            greet(at(-1, PANELS - 1 - p))

    @when(core == 1)
    def _():
        greet(at(-1, p))

    when(core == 0)(load_e.wait)
    when(core == 1)(load_o.wait)
    pl.semaphore_wait(barrier, jnp.where((core == 0) & edge, 2, 3))

    @when(core == 0)
    def _():
        loop(CHUNKS, lambda j: e_over(j).start())
        acc[...] = jnp.zeros_like(acc)

        def take(i):
            a, j = arrival(i)
            d_over(j).wait_recv()

            @when(passes(a))
            def _():
                d_pass(j, pass_to(a)).start()

            d_over(j).start()
            columns = pl.ds(pl.multiple_of(j * cols, cols), cols)
            er, ei = own[0], own[1]
            dr, di = drecv[j, 0], drecv[j, 1]
            gbuf[0, :, columns] = (dot(er, dr) - dot(ei, di)).astype(bf16)
            gbuf[1, :, columns] = (dot(er, di) + dot(ei, dr)).astype(bf16)

        def add(i):
            _, j = arrival(i)

            def rows_in(n):
                o_copy(j // 2, 2 * lax.rem(j, 2) + n, o_z, at(-3, p), o2buf, o2_recv).wait_recv()

            @when(site > 1)
            def _():
                loop(BANDS // 2, rows_in)

            columns = pl.ds(pl.multiple_of(j * cols, cols), cols)
            gr, gi = gbuf[0, :, columns], gbuf[1, :, columns]
            tr, ti = o2buf[0, columns, :], o2buf[1, columns, :]
            acc[0] += dot(gr, tr) - dot(gi, ti)
            acc[1] += dot(gr, ti) + dot(gi, tr)

        def added(i):
            return jnp.where(i < 3, 0, jnp.where(i < 6, 2 * i - 5, i))

        def step(i):
            take(i)

            def more(n, carry):
                add(n)
                return carry

            lax.fori_loop(added(i - 1), added(i), more, 0)

        def drain(i):
            a, j = arrival(i)
            d_over(j).wait_send()

            @when(passes(a))
            def _():
                d_pass(j, 1).wait_send()

        @when(site == 0)
        def _():
            out_ref[...] = own[...]

        @when(site > 0)
        def _():
            loop(CHUNKS, step)
            add(CHUNKS - 1)

            @when(site == 1)
            def _():
                out_ref[...] = gbuf[...]

            @when(site > 1)
            def _():
                out_ref[...] = acc[...].astype(bf16)

            loop(CHUNKS, drain)

        loop(CHUNKS, lambda j: e_over(j).wait_send())

    @when(core == 1)
    def _():
        def pass_o(q, c, right, left):
            @when(right & (p < PANELS - 1))
            def _():
                o_r(q, c).start()

            @when(left & (p > 0))
            def _():
                o_l(q, c).start()


            @when(site < sites - 2)
            def _():
                o_up(q, c).start()

        loop(BANDS, lambda c: pass_o(p, c, True, True))

        def hop(n):
            def one(c):
                @when(p - 1 - n >= 0)
                def _():
                    o_r(p - 1 - n, c).wait_recv()
                    pass_o(p - 1 - n, c, True, False)

                @when(p + 1 + n < PANELS)
                def _():
                    o_l(p + 1 + n, c).wait_recv()
                    pass_o(p + 1 + n, c, False, True)

            loop(BANDS, one)

        def own_e():
            loop(CHUNKS, lambda j: e_over(j).wait_recv())

        hop(0)
        own_e()

        @when(p == 0)
        def _():
            loop(CHUNKS, lambda j: e_r(0, j).start())

        @when(p == 3)
        def _():
            loop(CHUNKS, lambda j: e_l(3, CHUNKS - 1 - j).start())

        hop(1)

        @when(p == 1)
        def _():
            def one(j):
                e_r(1, j).start()
                e_r(0, j).wait_recv()
                e_r(0, j).start()

            loop(CHUNKS, one)

        @when(p == 2)
        def _():
            def one(i):
                j = CHUNKS - 1 - i
                e_l(2, j).start()
                e_l(3, j).wait_recv()
                e_l(3, j).start()

            loop(CHUNKS, one)

        hop(2)

        @when(p == 1)
        def _():
            def one(i):
                j = CHUNKS - 1 - i
                e_l(1, j).start()
                e_l(2, j).wait_recv()
                e_l(2, j).start()
                e_l(3, j).wait_recv()
                e_l(3, j).start()

            loop(CHUNKS, one)

        @when(p == 2)
        def _():
            def one(j):
                e_r(2, j).start()
                e_r(1, j).wait_recv()
                e_r(1, j).start()
                e_r(0, j).wait_recv()
                e_r(0, j).start()

            loop(CHUNKS, one)

        def nth(i):
            return jnp.where(p == 0, CHUNKS - 1 - i, i)

        def product(q, j):
            here = pl.ds(pl.multiple_of(q * rows, rows), rows)
            ar, ai = obuf[0, here, :], obuf[1, here, :]
            br, bi = ebuf[j, 0], ebuf[j, 1]
            re = (dot(ar, br) - dot(ai, bi)).astype(bf16)
            im = (dot(ar, bi) + dot(ai, br)).astype(bf16)
            return re, im

        @when(edge)
        def _():
            def one(i):
                j = nth(i)

                @when(p == 0)
                def _():
                    loop(PANELS - 1, lambda q: e_l(q + 1, j).wait_recv())

                @when(p == 3)
                def _():
                    loop(PANELS - 1, lambda q: e_r(q, j).wait_recv())

                def block(q):
                    here = pl.ds(pl.multiple_of(q * rows, rows), rows)
                    re, im = product(q, j)
                    dsend[j, 0, here, :] = re
                    dsend[j, 1, here, :] = im

                loop(PANELS, block)

                @when((i < direct_out) & (site < sites - 1))
                def _():
                    d_next(j).start()

                mine = pl.ds(pl.multiple_of(p * rows, rows), rows)
                columns = pl.ds(pl.multiple_of(j * cols, cols), cols)
                dloc[:, :, columns] = dsend[j, :, mine, :]

            loop(CHUNKS, one)

        @when(~edge)
        def _():
            def one(j):
                columns = pl.ds(pl.multiple_of(j * cols, cols), cols)
                re, im = product(p, j)
                dloc[0, :, columns] = re
                dloc[1, :, columns] = im

            loop(CHUNKS, one)

        def step(i):
            _, j = arrival(i)
            d_over(j).wait_recv()
            columns = pl.ds(pl.multiple_of(j * cols, cols), cols)
            ar, ai = dloc[0], dloc[1]
            br, bi = drecv[j, 0], drecv[j, 1]
            re = (dot(ar, br) - dot(ai, bi)).astype(bf16)
            im = (dot(ar, bi) + dot(ai, br)).astype(bf16)
            out_ref[0, :, columns] = re
            out_ref[1, :, columns] = im

        @when(site == 0)
        def _():
            out_ref[...] = dloc[...]

        @when(site > 0)
        def _():
            loop(CHUNKS, step)

        def drain_o(i):
            q, c = i // BANDS, lax.rem(i, BANDS)

            @when(site < sites - 2)
            def _():
                o_up(q, c).wait_send()

            @when((q <= p) & (p < PANELS - 1))
            def _():
                o_r(q, c).wait_send()

            @when((q >= p) & (p > 0))
            def _():
                o_l(q, c).wait_send()

        loop(PANELS * BANDS, drain_o)

        def drain_e(i):
            q, j = i // CHUNKS, lax.rem(i, CHUNKS)

            @when((q <= p) & (p < PANELS - 1))
            def _():
                e_r(q, j).wait_send()

            @when((q >= p) & (p > 0))
            def _():
                e_l(q, j).wait_send()

        loop(PANELS * CHUNKS, drain_e)

        @when(edge)
        def _():
            def drain_d(i):
                @when((i < direct_out) & (site < sites - 1))
                def _():
                    d_next(nth(i)).wait_send()

            loop(CHUNKS, drain_d)


def shards(forward_props):
    x = forward_props[:, 0]
    _, rows, width = x.shape
    cols = width // CHUNKS
    dma = pltpu.SemaphoreType.DMA
    tm_size = lax.axis_size("tm")
    out = pl.pallas_call(
        functools.partial(kernel, tm_size),
        out_shape=jax.ShapeDtypeStruct(x.shape, bf16),
        in_specs=[pl.BlockSpec(memory_space=pl.ANY)],
        out_specs=pl.BlockSpec(memory_space=pltpu.VMEM),
        scratch_shapes=[
            pltpu.VMEM(x.shape, bf16),
            pltpu.VMEM((2, width, width), bf16),
            pltpu.VMEM((2, width, width), bf16),
            pltpu.VMEM((CHUNKS, 2, width, cols), bf16),
            pltpu.VMEM((CHUNKS, 2, width, cols), bf16),
            pltpu.VMEM((CHUNKS, 2, width, cols), bf16),
            pltpu.VMEM(x.shape, bf16),
            pltpu.VMEM(x.shape, bf16),
            pltpu.VMEM(x.shape, f32),
            dma,
            dma((PANELS, BANDS)),
            dma((PANELS, BANDS)),
            dma((PANELS, BANDS)),
            dma((PANELS, BANDS)),
            dma((PANELS, BANDS)),
            dma((PANELS, CHUNKS)),
            dma((PANELS, CHUNKS)),
            dma((PANELS, CHUNKS)),
            dma((CHUNKS,)),
            dma((CHUNKS,)),
            dma((CHUNKS,)),
            dma((CHUNKS,)),
        ],
        compiler_params=pltpu.CompilerParams(
            collective_id=0, has_side_effects=True, vmem_limit_bytes=48 * 2**20
        ),
        name="prefix_products",
    )(x)
    return out[:, None]


def solution(mesh):
    placed = (P(None, "tm", "panel", None),)
    return jax.shard_map(
        shards, mesh=mesh, in_specs=placed, out_specs=P(None, "tm", "panel", None), check_vma=False
    )
```

```python
import functools

import jax
import jax.numpy as jnp
from jax import lax
from jax.experimental import pallas as pl
from jax.experimental.pallas import tpu as pltpu
from jax.sharding import PartitionSpec as P

PANELS = 4
CHUNKS = 8
EARLY = 4
BANDS = 4

bf16, f32 = jnp.bfloat16, jnp.float32


def dot(a, b):
    return jnp.dot(a, b, preferred_element_type=f32)


def when(cond):
    return pl.when(cond)


def loop(n, body):
    def step(i, carry):
        body(i)
        return carry

    lax.fori_loop(0, n, step, 0)


def kernel(
    tm_size, x_ref, out_ref, own, obuf, o2buf, ebuf, dsend, drecv, dloc, gbuf, acc,
    in_sem, o_recv, o_right, o_left, o_z, o2_recv, e_recv, e_right, e_left, e_in, d_recv, d_out, d_in,
    relay, relay_recv, relay_out, rows_recv, rows_out,
):
    rows, width = x_ref.shape[1], x_ref.shape[2]
    cols = width // CHUNKS
    band = rows // BANDS
    tm, p = lax.axis_index("tm"), lax.axis_index("panel")
    core = lax.rem(tm, 2)
    site, sites = tm // 2, tm_size // 2

    def at(shift, panel):
        return (lax.rem(tm + shift + tm_size, tm_size), panel)

    def remote(src, dst, send, recv, where):
        return pltpu.make_async_remote_copy(
            src_ref=src, dst_ref=dst, send_sem=send, recv_sem=recv,
            device_id=where, device_id_type=pl.DeviceIdType.MESH,
        )

    def o_rows(q, c):
        return pl.ds(pl.multiple_of(q * rows + c * band, band), band)

    def o_copy(q, c, sems, where, dst=None, recv=None):
        piece = obuf.at[:, o_rows(q, c), :]
        target = piece if dst is None else dst.at[:, o_rows(q, c), :]
        arrive = (o_recv if recv is None else recv).at[q, c]
        return remote(piece, target, sems.at[q, c], arrive, where)

    def o_r(q, c):
        return o_copy(q, c, o_right, at(0, lax.rem(p + 1, PANELS)))

    def o_l(q, c):
        return o_copy(q, c, o_left, at(0, lax.rem(p + PANELS - 1, PANELS)))

    def o_up(q, c):
        return o_copy(q, c, o_z, at(3, p), o2buf, o2_recv)

    def o_aside(c):
        here = pl.ds(pl.multiple_of(c * band, band), band)
        return remote(
            obuf.at[:, o_rows(p, c), :], relay.at[:, here, :], o_z.at[p, c], relay_recv.at[c], at(5, PANELS - 1 - p)
        )

    def o_aside_on(c):
        here = pl.ds(pl.multiple_of(c * band, band), band)
        q = PANELS - 1 - p
        return remote(relay.at[:, here, :], o2buf.at[:, o_rows(q, c), :], relay_out.at[c], o2_recv.at[q, c], at(-2, q))

    def e_piece(q, j):
        return ebuf.at[j, :, pl.ds(pl.multiple_of(q * rows, rows), rows), :]

    def e_copy(q, j, sems, panel):
        return remote(e_piece(q, j), e_piece(q, j), sems.at[q, j], e_recv.at[q, j], at(0, panel))

    def e_r(q, j):
        return e_copy(q, j, e_right, lax.rem(p + 1, PANELS))

    def e_l(q, j):
        return e_copy(q, j, e_left, lax.rem(p + PANELS - 1, PANELS))

    def e_over(j):
        columns = pl.ds(pl.multiple_of(j * cols, cols), cols)
        return remote(own.at[:, :, columns], e_piece(p, j), e_in.at[j], e_recv.at[p, j], at(1, p))

    def d_next(j):
        return remote(dsend.at[j], drecv.at[j], d_out.at[j], d_recv.at[j], at(1, PANELS - 1 - p))

    def d_pass(j, panel):
        return remote(drecv.at[j], drecv.at[j], d_out.at[j], d_recv.at[j], at(0, panel))

    def d_over(j):
        return remote(drecv.at[j], drecv.at[j], d_in.at[j], d_recv.at[j], at(1, p))

    def piece(half, g, k, n):
        first = 2 * g
        q = jnp.where(half == 0, PANELS - 1 - k, k)
        j = jnp.where(half == 0, first, CHUNKS - first - n)
        return pl.ds(j, n), slice(None), pl.ds(pl.multiple_of(q * rows, rows), rows), slice(None)

    def rows_next(half, g, k):
        view = piece(half, g, k, 2)
        m = PANELS * g + k
        return remote(
            dsend.at[view], drecv.at[view], rows_out.at[half, m], rows_recv.at[half, m], at(1, PANELS - 1 - p)
        )

    def rows_pass(half, g, k, n, panel):
        view = piece(half, g, k, n)
        m = PANELS * g + k
        return remote(drecv.at[view], drecv.at[view], rows_out.at[half, m], rows_recv.at[half, m], at(0, panel))

    odd = lax.rem(site, 2) == 1
    direct_out = jnp.where(odd, 6, 7)
    direct_in = jnp.where(odd, 7, 6)
    edge = (p == 0) | (p == PANELS - 1)
    low = p < PANELS // 2

    def pick(i, values):
        found = values[-1]
        for n in range(len(values) - 1):
            found = jnp.where(i == n, values[n], found)
        return found

    def arrival(i):
        inner = jnp.where(odd, pick(i, (0, 1, 7, 2, 6, 3, 5, 4)), pick(i, (0, 1, 2, 3, 7, 6, 5, 4)))
        outer = pick(i, (0, 1, 2, 3, 4, 7, 6, 5))
        a = jnp.where(edge, outer, inner)
        j = jnp.where(low, a, CHUNKS - 1 - a)
        return a, j

    def passes(a):
        return jnp.where(edge, a < 5, (a < 3) | (a >= direct_in))

    def pass_to(a):
        onward = jnp.where(edge, jnp.where(low, 1, 2), jnp.where(low, 2, 1))
        back = jnp.where(low, 0, PANELS - 1)
        return jnp.where(~edge & (a >= direct_in), back, onward)

    load_e = pltpu.make_async_copy(x_ref, own, in_sem)
    load_o = pltpu.make_async_copy(x_ref, obuf.at[:, pl.ds(pl.multiple_of(p * rows, rows), rows), :], in_sem)
    when(core == 0)(load_e.start)
    when(core == 1)(load_o.start)

    barrier = pltpu.get_barrier_semaphore()

    def greet(where):
        pl.semaphore_signal(barrier, inc=1, device_id=where, device_id_type=pl.DeviceIdType.MESH)

    @when(p > 0)
    def _():
        greet(at(0, p - 1))

    @when(p < PANELS - 1)
    def _():
        greet(at(0, p + 1))

    @when(core == 0)
    def _():
        greet(at(-3, p))

        @when(edge)
        def _():
            greet(at(-1, PANELS - 1 - p))

        @when(edge & odd)
        def _():
            greet(at(-5, PANELS - 1 - p))

        @when(edge & ~odd)
        def _():
            greet(at(2, PANELS - 1 - p))

    @when(core == 1)
    def _():
        greet(at(-1, p))

    when(core == 0)(load_e.wait)
    when(core == 1)(load_o.wait)
    pl.semaphore_wait(barrier, jnp.where(edge & ~odd, jnp.where(core == 0, 2, 4), 3))

    @when(core == 0)
    def _():
        loop(CHUNKS, lambda j: e_over(j).start())
        acc[...] = jnp.zeros_like(acc)

        @when(edge & odd & (site > 2))
        def _():
            def hand_on(c):
                o_aside(c).wait_recv()
                o_aside_on(c).start()

            loop(BANDS, hand_on)

        def take(i):
            come(i)
            multiply(i)

        def come(i):
            a, j = arrival(i)
            d_over(j).wait_recv()

            @when(passes(a))
            def _():
                d_pass(j, pass_to(a)).start()

            d_over(j).start()

        def multiply(i):
            _, j = arrival(i)
            columns = pl.ds(pl.multiple_of(j * cols, cols), cols)
            er, ei = own[0], own[1]
            dr, di = drecv[j, 0], drecv[j, 1]
            gbuf[0, :, columns] = (dot(er, dr) - dot(ei, di)).astype(bf16)
            gbuf[1, :, columns] = (dot(er, di) + dot(ei, dr)).astype(bf16)

        def add(i, final=False):
            _, j = arrival(i)

            def rows_in(n):
                o_copy(j // 2, 2 * lax.rem(j, 2) + n, o_z, at(-3, p), o2buf, o2_recv).wait_recv()

            loop(BANDS // 2, rows_in)
            columns = pl.ds(pl.multiple_of(j * cols, cols), cols)
            gr, gi = gbuf[0, :, columns], gbuf[1, :, columns]
            tr, ti = o2buf[0, columns, :], o2buf[1, columns, :]
            re = acc[0] + (dot(gr, tr) - dot(gi, ti))
            im = acc[1] + (dot(gr, ti) + dot(gi, tr))
            if final:
                out_ref[0] = re.astype(bf16)
                out_ref[1] = im.astype(bf16)
            else:
                acc[0] = re
                acc[1] = im

        def pair_of(g):
            return jnp.where(low, 2 * g, CHUNKS - 2 - 2 * g)

        def multiply_pair(g):
            j = pair_of(g)
            columns = pl.ds(pl.multiple_of(j * cols, cols), 2 * cols)
            er, ei = own[0], own[1]
            dr = jnp.concatenate([drecv[j, 0], drecv[j + 1, 0]], axis=1)
            di = jnp.concatenate([drecv[j, 1], drecv[j + 1, 1]], axis=1)
            gbuf[0, :, columns] = (dot(er, dr) - dot(ei, di)).astype(bf16)
            gbuf[1, :, columns] = (dot(er, di) + dot(ei, dr)).astype(bf16)

        def add_pair(g, final=False):
            j = pair_of(g)
            loop(BANDS, lambda c: o_copy(j // 2, c, o_z, at(-3, p), o2buf, o2_recv).wait_recv())
            columns = pl.ds(pl.multiple_of(j * cols, cols), 2 * cols)
            gr, gi = gbuf[0, :, columns], gbuf[1, :, columns]
            tr, ti = o2buf[0, columns, :], o2buf[1, columns, :]
            re = acc[0] + (dot(gr, tr) - dot(gi, ti))
            im = acc[1] + (dot(gr, ti) + dot(gi, tr))
            if final:
                out_ref[0] = re.astype(bf16)
                out_ref[1] = im.astype(bf16)
            else:
                acc[0] = re
                acc[1] = im

        def added(i):
            return jnp.where(i < 3, 0, jnp.where(i < 6, 2 * i - 5, i))

        def step(i):
            take(i)

            def more(n, carry):
                add(n)
                return carry

            @when(site > 1)
            def _():
                lax.fori_loop(added(i - 1), added(i), more, 0)

        def drain(i):
            a, j = arrival(i)
            d_over(j).wait_send()

            @when(passes(a))
            def _():
                d_pass(j, 1).wait_send()

        main = jnp.where(low, 0, 1)
        other = 1 - main

        def span(first, end, f):
            loop(end - first, lambda i: f(first + i))

        def take_rows(k):
            @when(edge)
            def _():
                for g in range(2):
                    rows_pass(main, g, k, 2, pass_to(0)).wait_recv()
                    rows_pass(main, g, k, 2, pass_to(0)).start()

                @when(k > 0)
                def _():
                    rows_pass(other, 0, k - 1, 2, pass_to(0)).wait_recv()

            @when(~edge)
            def _():
                for g in range(2):
                    rows_pass(main, g, k, 2, pass_to(0)).wait_recv()
                    rows_pass(main, g, k, 2 - g, pass_to(0)).start()
                for g in range(2):
                    rows_pass(other, g, k, 2 - g, pass_to(0)).wait_recv()
                    if g == 0:
                        rows_pass(other, g, k, 2, pass_to(7)).start()

        def drain_rows(k):
            rows_pass(main, 0, k, 2, pass_to(0)).wait_send()

            @when(edge)
            def _():
                rows_pass(main, 1, k, 2, pass_to(0)).wait_send()

            @when(~edge)
            def _():
                rows_pass(main, 1, k, 1, pass_to(0)).wait_send()
                rows_pass(other, 0, k, 2, pass_to(7)).wait_send()

        def over(i):
            d_over(arrival(i)[1]).start()

        @when(site == 0)
        def _():
            out_ref[...] = own[...]

        @when((site > 0) & odd)
        def _():
            loop(CHUNKS, step)
            loop(CHUNKS, drain)

        @when((site > 0) & ~odd)
        def _():
            loop(PANELS, take_rows)
            span(0, 4, over)

            @when(~edge)
            def _():
                span(4, 7, over)

            loop(2, multiply_pair)

            @when(edge)
            def _():
                come(4)
                loop(2, add_pair)
                rows_pass(other, 0, PANELS - 1, 2, pass_to(0)).wait_recv()
                span(5, 7, over)

            multiply_pair(3)

            @when(~edge)
            def _():
                come(7)
                loop(2, add_pair)

            add_pair(3)

            @when(edge)
            def _():
                come(7)

            multiply_pair(2)
            add_pair(2, final=True)

        @when(site == 1)
        def _():
            out_ref[...] = gbuf[...]

        @when((site > 1) & odd)
        def _():
            add(CHUNKS - 1, final=True)

        @when((site > 0) & ~odd)
        def _():
            loop(PANELS, drain_rows)
            loop(CHUNKS, lambda j: d_over(j).wait_send())

            @when(edge)
            def _():
                d_pass(arrival(4)[1], 1).wait_send()

        loop(CHUNKS, lambda j: e_over(j).wait_send())

        @when(edge & odd & (site > 2))
        def _():
            loop(BANDS, lambda c: o_aside_on(c).wait_send())

    @when(core == 1)
    def _():
        def pass_o(q, c, right, left):
            @when(right & (p < PANELS - 1))
            def _():
                o_r(q, c).start()

            @when(left & (p > 0))
            def _():
                o_l(q, c).start()

            aside = edge & ~odd & (q == p)

            @when((site < sites - 2) & ~aside)
            def _():
                o_up(q, c).start()

            @when((site < sites - 2) & aside)
            def _():
                o_aside(c).start()

        def hop(n):
            def one(c):
                @when(p - 1 - n >= 0)
                def _():
                    o_r(p - 1 - n, c).wait_recv()
                    pass_o(p - 1 - n, c, True, False)

                @when(p + 1 + n < PANELS)
                def _():
                    o_l(p + 1 + n, c).wait_recv()
                    pass_o(p + 1 + n, c, False, True)

            loop(BANDS, one)

        def own_e():
            loop(CHUNKS, lambda j: e_over(j).wait_recv())

        def nth(i):
            return jnp.where(p == 0, CHUNKS - 1 - i, i)

        def product(q, j):
            here = pl.ds(pl.multiple_of(q * rows, rows), rows)
            ar, ai = obuf[0, here, :], obuf[1, here, :]
            br, bi = ebuf[j, 0], ebuf[j, 1]
            re = (dot(ar, br) - dot(ai, bi)).astype(bf16)
            im = (dot(ar, bi) + dot(ai, br)).astype(bf16)
            return re, im

        def two(j, part):
            return jnp.concatenate([ebuf[j, part], ebuf[j + 1, part]], axis=1)

        def rows_of(q, j):
            here = pl.ds(pl.multiple_of(q * rows, rows), rows)
            ar, ai = obuf[0, here, :], obuf[1, here, :]
            br, bi = two(j, 0), two(j, 1)
            re = (dot(ar, br) - dot(ai, bi)).astype(bf16)
            im = (dot(ar, bi) + dot(ai, br)).astype(bf16)
            for n in range(2):
                dsend[j + n, 0, here, :] = re[:, n * cols : (n + 1) * cols]
                dsend[j + n, 1, here, :] = im[:, n * cols : (n + 1) * cols]

        def e_in_chunk(j):
            @when(p == 0)
            def _():
                loop(PANELS - 1, lambda q: e_l(q + 1, j).wait_recv())

            @when(p == 3)
            def _():
                loop(PANELS - 1, lambda q: e_r(q, j).wait_recv())

        def copy_own(j):
            mine = pl.ds(pl.multiple_of(p * rows, rows), rows)
            dloc[:, :, pl.ds(pl.multiple_of(j * cols, cols), cols)] = dsend[j, :, mine, :]

        def own_chunk(j):
            columns = pl.ds(pl.multiple_of(j * cols, cols), cols)
            re, im = product(p, j)
            dloc[0, :, columns] = re
            dloc[1, :, columns] = im

        def whole_chunk(i):
            j = nth(i)
            e_in_chunk(j)

            def block(q):
                here = pl.ds(pl.multiple_of(q * rows, rows), rows)
                re, im = product(q, j)
                dsend[j, 0, here, :] = re
                dsend[j, 1, here, :] = im

            @when(i < direct_out)
            def _():
                loop(PANELS, block)

                @when(site < sites - 1)
                def _():
                    d_next(j).start()

                copy_own(j)

            @when(i >= direct_out)
            def _():
                own_chunk(j)

        @when(~odd)
        def _():
            loop(BANDS, lambda c: pass_o(p, c, True, True))
            hop(0)
            own_e()

            @when(p == 0)
            def _():
                loop(CHUNKS, lambda j: e_r(0, j).start())

            @when(p == 3)
            def _():
                loop(CHUNKS, lambda j: e_l(3, CHUNKS - 1 - j).start())

            hop(1)

            @when(p == 1)
            def _():
                def one(j):
                    e_r(1, j).start()
                    e_r(0, j).wait_recv()
                    e_r(0, j).start()

                loop(CHUNKS, one)

            @when(p == 2)
            def _():
                def one(i):
                    j = CHUNKS - 1 - i
                    e_l(2, j).start()
                    e_l(3, j).wait_recv()
                    e_l(3, j).start()

                loop(CHUNKS, one)

            hop(2)

            @when(p == 1)
            def _():
                def one(i):
                    j = CHUNKS - 1 - i
                    e_l(1, j).start()
                    e_l(2, j).wait_recv()
                    e_l(2, j).start()
                    e_l(3, j).wait_recv()
                    e_l(3, j).start()

                loop(CHUNKS, one)

            @when(p == 2)
            def _():
                def one(j):
                    e_r(2, j).start()
                    e_r(1, j).wait_recv()
                    e_r(1, j).start()
                    e_r(0, j).wait_recv()
                    e_r(0, j).start()

                loop(CHUNKS, one)

            @when(edge)
            def _():
                loop(CHUNKS, whole_chunk)

        def pair(q, j, sems, panel):
            view = ebuf.at[pl.ds(j, 2), :, pl.ds(pl.multiple_of(q * rows, rows), rows), :]
            return remote(view, view, sems.at[q, j], e_recv.at[q, j], at(0, panel))

        def pair_r(q, b):
            return pair(q, 2 * b, e_right, lax.rem(p + 1, PANELS))

        def pair_l(q, b):
            return pair(q, CHUNKS - 2 - 2 * b, e_left, lax.rem(p + PANELS - 1, PANELS))

        sent = jnp.where(p == 0, 1, 0)

        @when(odd)
        def _():
            def pass_e(q, b, right, left):
                @when(right & (p < PANELS - 1))
                def _():
                    pair_r(q, b).start()

                @when(left & (p > 0))
                def _():
                    pair_l(q, b).start()

            def own_o(n):
                def one(c):
                    @when((p == n) & (p < PANELS - 1))
                    def _():
                        o_r(p, c).start()

                    @when((p == PANELS - 1 - n) & (p > 0))
                    def _():
                        o_l(p, c).start()

                loop(BANDS, one)

            @when(site < sites - 2)
            def _():
                loop(BANDS, lambda c: o_up(p, c).start())

            own_e()
            for b in range(EARLY // 2):
                pass_e(p, b, True, True)
            own_o(0)
            for n in range(PANELS - 1):
                def one(b):
                    @when(p - 1 - n >= 0)
                    def _():
                        pair_r(p - 1 - n, b).wait_recv()
                        pass_e(p - 1 - n, b, True, False)

                    @when(p + 1 + n < PANELS)
                    def _():
                        pair_l(p + 1 + n, b).wait_recv()
                        pass_e(p + 1 + n, b, False, True)

                loop(EARLY // 2, one)
                own_o(n + 1)

            def send_rows(k):
                @when(edge)
                def _():
                    for g in range(2):
                        rows_of(jnp.where(p == 0, k, PANELS - 1 - k), jnp.where(p == 0, CHUNKS - 2 - 2 * g, 2 * g))

                        @when(site < sites - 1)
                        def _():
                            rows_next(sent, g, k).start()

            send_rows(0)
            hop(0)
            send_rows(1)

            @when(p == 0)
            def _():
                loop(EARLY, lambda i: e_r(0, EARLY + i).start())

            @when(p == 3)
            def _():
                loop(EARLY, lambda i: e_l(3, EARLY - 1 - i).start())

            hop(1)
            send_rows(2)

            @when(p == 1)
            def _():
                def one(i):
                    j = EARLY + i
                    e_r(1, j).start()
                    e_r(0, j).wait_recv()
                    e_r(0, j).start()

                loop(EARLY, one)

            @when(p == 2)
            def _():
                def one(i):
                    j = EARLY - 1 - i
                    e_l(2, j).start()
                    e_l(3, j).wait_recv()
                    e_l(3, j).start()

                loop(EARLY, one)

            hop(2)
            send_rows(3)

            @when(p == 1)
            def _():
                def one(i):
                    j = EARLY - 1 - i
                    e_l(1, j).start()
                    e_l(2, j).wait_recv()
                    e_l(2, j).start()
                    e_l(3, j).wait_recv()
                    e_l(3, j).start()

                loop(EARLY, one)

            @when(p == 2)
            def _():
                def one(i):
                    j = EARLY + i
                    e_r(2, j).start()
                    e_r(1, j).wait_recv()
                    e_r(1, j).start()
                    e_r(0, j).wait_recv()
                    e_r(0, j).start()

                loop(EARLY, one)

            @when(edge)
            def _():
                loop(EARLY, lambda i: whole_chunk(EARLY + i))
                loop(EARLY, lambda i: copy_own(nth(i)))

        @when(~edge)
        def _():
            loop(CHUNKS, own_chunk)

        def step(i):
            _, j = arrival(i)
            d_over(j).wait_recv()
            columns = pl.ds(pl.multiple_of(j * cols, cols), cols)
            ar, ai = dloc[0], dloc[1]
            br, bi = drecv[j, 0], drecv[j, 1]
            re = (dot(ar, br) - dot(ai, bi)).astype(bf16)
            im = (dot(ar, bi) + dot(ai, br)).astype(bf16)
            out_ref[0, :, columns] = re
            out_ref[1, :, columns] = im

        @when(site == 0)
        def _():
            out_ref[...] = dloc[...]

        def step_pair(i):
            g = pick(i, (0, 1, 3, 2))
            j = jnp.where(low, 2 * g, CHUNKS - 2 - 2 * g)
            loop(2, lambda n: d_over(j + n).wait_recv())
            columns = pl.ds(pl.multiple_of(j * cols, cols), 2 * cols)
            ar, ai = dloc[0], dloc[1]
            br = jnp.concatenate([drecv[j, 0], drecv[j + 1, 0]], axis=1)
            bi = jnp.concatenate([drecv[j, 1], drecv[j + 1, 1]], axis=1)
            out_ref[0, :, columns] = (dot(ar, br) - dot(ai, bi)).astype(bf16)
            out_ref[1, :, columns] = (dot(ar, bi) + dot(ai, br)).astype(bf16)

        @when((site > 0) & ~odd)
        def _():
            loop(CHUNKS // 2, step_pair)

        @when((site > 0) & odd)
        def _():
            loop(CHUNKS, step)

        def drain_o(i):
            q, c = i // BANDS, lax.rem(i, BANDS)

            @when(site < sites - 2)
            def _():
                o_up(q, c).wait_send()

            @when((q <= p) & (p < PANELS - 1))
            def _():
                o_r(q, c).wait_send()

            @when((q >= p) & (p > 0))
            def _():
                o_l(q, c).wait_send()

        loop(PANELS * BANDS, drain_o)

        def drain_e(i):
            q, j = i // CHUNKS, lax.rem(i, CHUNKS)

            @when((q <= p) & (p < PANELS - 1))
            def _():
                @when(~odd | (j >= EARLY))
                def _():
                    e_r(q, j).wait_send()

                @when(odd & (j < EARLY // 2))
                def _():
                    pair_r(q, j).wait_send()

            @when((q >= p) & (p > 0))
            def _():
                @when(~odd | (j < EARLY))
                def _():
                    e_l(q, j).wait_send()

                @when(odd & (j >= EARLY) & (j < EARLY + EARLY // 2))
                def _():
                    pair_l(q, j - EARLY).wait_send()

        loop(PANELS * CHUNKS, drain_e)

        @when(edge)
        def _():
            def drain_d(i):
                @when((i < direct_out) & (site < sites - 1) & (~odd | (i >= EARLY)))
                def _():
                    d_next(nth(i)).wait_send()

            loop(CHUNKS, drain_d)

            @when(odd & (site < sites - 1))
            def _():
                for g in range(2):
                    loop(PANELS, lambda k: rows_next(sent, g, k).wait_send())


def shards(forward_props):
    x = forward_props[:, 0]
    _, rows, width = x.shape
    cols = width // CHUNKS
    dma = pltpu.SemaphoreType.DMA
    tm_size = lax.axis_size("tm")
    out = pl.pallas_call(
        functools.partial(kernel, tm_size),
        out_shape=jax.ShapeDtypeStruct(x.shape, bf16),
        in_specs=[pl.BlockSpec(memory_space=pl.ANY)],
        out_specs=pl.BlockSpec(memory_space=pltpu.VMEM),
        scratch_shapes=[
            pltpu.VMEM(x.shape, bf16),
            pltpu.VMEM((2, width, width), bf16),
            pltpu.VMEM((2, width, width), bf16),
            pltpu.VMEM((CHUNKS, 2, width, cols), bf16),
            pltpu.VMEM((CHUNKS, 2, width, cols), bf16),
            pltpu.VMEM((CHUNKS, 2, width, cols), bf16),
            pltpu.VMEM(x.shape, bf16),
            pltpu.VMEM(x.shape, bf16),
            pltpu.VMEM(x.shape, f32),
            dma,
            dma((PANELS, BANDS)),
            dma((PANELS, BANDS)),
            dma((PANELS, BANDS)),
            dma((PANELS, BANDS)),
            dma((PANELS, BANDS)),
            dma((PANELS, CHUNKS)),
            dma((PANELS, CHUNKS)),
            dma((PANELS, CHUNKS)),
            dma((CHUNKS,)),
            dma((CHUNKS,)),
            dma((CHUNKS,)),
            dma((CHUNKS,)),
            pltpu.VMEM(x.shape, bf16),
            dma((BANDS,)),
            dma((BANDS,)),
            dma((2, 2 * PANELS)),
            dma((2, 2 * PANELS)),
        ],
        compiler_params=pltpu.CompilerParams(
            collective_id=0, has_side_effects=True, vmem_limit_bytes=52 * 2**20
        ),
        name="prefix_products",
    )(x)
    return out[:, None]


def solution(mesh):
    placed = (P(None, "tm", "panel", None),)
    return jax.shard_map(
        shards, mesh=mesh, in_specs=placed, out_specs=P(None, "tm", "panel", None), check_vma=False
    )
```

```python
import functools

import jax
import jax.numpy as jnp
from jax import lax
from jax.experimental import pallas as pl
from jax.experimental.pallas import tpu as pltpu
from jax.sharding import PartitionSpec as P

PANELS = 4
CHUNKS = 8
EARLY = 4
BANDS = 4

bf16, f32 = jnp.bfloat16, jnp.float32


def dot(a, b):
    return jnp.dot(a, b, preferred_element_type=f32)


def when(cond):
    return pl.when(cond)


def loop(n, body):
    def step(i, carry):
        body(i)
        return carry

    lax.fori_loop(0, n, step, 0)


def kernel(
    tm_size, x_ref, out_ref, own, obuf, o2buf, ebuf, dsend, drecv, dloc, gbuf, acc,
    in_sem, o_recv, o_right, o_left, o_z, o2_recv, e_recv, e_right, e_left, e_in, d_recv, d_out, d_in,
    relay, relay_recv, relay_out, rows_recv, rows_out, wide,
):
    rows, width = x_ref.shape[1], x_ref.shape[2]
    cols = width // CHUNKS
    band = rows // BANDS
    tm, p = lax.axis_index("tm"), lax.axis_index("panel")
    core = lax.rem(tm, 2)
    site, sites = tm // 2, tm_size // 2

    def at(shift, panel):
        return (lax.rem(tm + shift + tm_size, tm_size), panel)

    def remote(src, dst, send, recv, where):
        return pltpu.make_async_remote_copy(
            src_ref=src, dst_ref=dst, send_sem=send, recv_sem=recv,
            device_id=where, device_id_type=pl.DeviceIdType.MESH,
        )

    def o_rows(q, c):
        return pl.ds(pl.multiple_of(q * rows + c * band, band), band)

    def o_copy(q, c, sems, where, dst=None, recv=None):
        piece = obuf.at[:, o_rows(q, c), :]
        target = piece if dst is None else dst.at[:, o_rows(q, c), :]
        arrive = (o_recv if recv is None else recv).at[q, c]
        return remote(piece, target, sems.at[q, c], arrive, where)

    def o_r(q, c):
        return o_copy(q, c, o_right, at(0, lax.rem(p + 1, PANELS)))

    def o_l(q, c):
        return o_copy(q, c, o_left, at(0, lax.rem(p + PANELS - 1, PANELS)))

    def o_up(q, c):
        return o_copy(q, c, o_z, at(3, p), o2buf, o2_recv)

    def o_aside(c):
        here = pl.ds(pl.multiple_of(c * band, band), band)
        return remote(
            obuf.at[:, o_rows(p, c), :], relay.at[:, here, :], o_z.at[p, c], relay_recv.at[c], at(5, PANELS - 1 - p)
        )

    def o_aside_on(c):
        here = pl.ds(pl.multiple_of(c * band, band), band)
        q = PANELS - 1 - p
        return remote(relay.at[:, here, :], o2buf.at[:, o_rows(q, c), :], relay_out.at[c], o2_recv.at[q, c], at(-2, q))

    def e_piece(q, j):
        return ebuf.at[j, :, pl.ds(pl.multiple_of(q * rows, rows), rows), :]

    def e_copy(q, j, sems, panel):
        return remote(e_piece(q, j), e_piece(q, j), sems.at[q, j], e_recv.at[q, j], at(0, panel))

    def e_r(q, j):
        return e_copy(q, j, e_right, lax.rem(p + 1, PANELS))

    def e_l(q, j):
        return e_copy(q, j, e_left, lax.rem(p + PANELS - 1, PANELS))

    def e_over(j):
        return remote(e_piece(p, j), e_piece(p, j), e_in.at[j], e_recv.at[p, j], at(1, p))

    def pair(q, j, sems, shift, panel):
        view = ebuf.at[pl.ds(j, 2), :, pl.ds(pl.multiple_of(q * rows, rows), rows), :]
        return remote(view, view, sems.at[q, j], e_recv.at[q, j], at(shift, panel))

    def pair_r(q, b, shift=0):
        return pair(q, 2 * b, e_right, shift, lax.rem(p + 1, PANELS))

    def pair_l(q, b, shift=0):
        return pair(q, CHUNKS - 2 - 2 * b, e_left, shift, lax.rem(p + PANELS - 1, PANELS))

    def d_next(j):
        return remote(dsend.at[j], drecv.at[j], d_out.at[j], d_recv.at[j], at(1, PANELS - 1 - p))

    def d_pass(j, panel):
        return remote(drecv.at[j], drecv.at[j], d_out.at[j], d_recv.at[j], at(0, panel))

    def d_over(j):
        return remote(drecv.at[j], drecv.at[j], d_in.at[j], d_recv.at[j], at(1, p))

    def piece(half, g, k, n):
        first = 2 * g
        q = jnp.where(half == 0, PANELS - 1 - k, k)
        j = jnp.where(half == 0, first, CHUNKS - first - n)
        return pl.ds(j, n), slice(None), pl.ds(pl.multiple_of(q * rows, rows), rows), slice(None)

    def rows_next(half, g, k):
        view = piece(half, g, k, 2)
        m = PANELS * g + k
        return remote(
            dsend.at[view], drecv.at[view], rows_out.at[half, m], rows_recv.at[half, m], at(1, PANELS - 1 - p)
        )

    def rows_pass(half, g, k, n, panel):
        view = piece(half, g, k, n)
        m = PANELS * g + k
        return remote(drecv.at[view], drecv.at[view], rows_out.at[half, m], rows_recv.at[half, m], at(0, panel))

    odd = lax.rem(site, 2) == 1
    direct_out = jnp.where(odd, 6, 7)
    direct_in = jnp.where(odd, 7, 6)
    edge = (p == 0) | (p == PANELS - 1)
    low = p < PANELS // 2

    def pick(i, values):
        found = values[-1]
        for n in range(len(values) - 1):
            found = jnp.where(i == n, values[n], found)
        return found

    def arrival(i):
        inner = jnp.where(odd, pick(i, (0, 1, 7, 2, 6, 3, 5, 4)), pick(i, (0, 1, 2, 3, 7, 6, 5, 4)))
        outer = pick(i, (0, 1, 2, 3, 4, 7, 6, 5))
        a = jnp.where(edge, outer, inner)
        j = jnp.where(low, a, CHUNKS - 1 - a)
        return a, j

    def passes(a):
        return jnp.where(edge, a < 5, (a < 3) | (a >= direct_in))

    def pass_to(a):
        onward = jnp.where(edge, jnp.where(low, 1, 2), jnp.where(low, 2, 1))
        back = jnp.where(low, 0, PANELS - 1)
        return jnp.where(~edge & (a >= direct_in), back, onward)

    def load_chunk(j):
        columns = pl.ds(pl.multiple_of(j * cols, cols), cols)
        return pltpu.make_async_copy(x_ref.at[:, :, columns], e_piece(p, j), in_sem.at[j])

    load_e = pltpu.make_async_copy(x_ref, own, in_sem.at[CHUNKS])
    load_o = pltpu.make_async_copy(
        x_ref, obuf.at[:, pl.ds(pl.multiple_of(p * rows, rows), rows), :], in_sem.at[CHUNKS]
    )

    @when(core == 0)
    def _():
        loop(CHUNKS, lambda j: load_chunk(j).start())
        load_e.start()

    when(core == 1)(load_o.start)

    barrier = pltpu.get_barrier_semaphore()

    def greet(where):
        pl.semaphore_signal(barrier, inc=1, device_id=where, device_id_type=pl.DeviceIdType.MESH)

    @when(p > 0)
    def _():
        greet(at(0, p - 1))

    @when(p < PANELS - 1)
    def _():
        greet(at(0, p + 1))

    @when(core == 0)
    def _():
        greet(at(-3, p))

        @when(edge)
        def _():
            greet(at(-1, PANELS - 1 - p))

        @when(edge & odd)
        def _():
            greet(at(-5, PANELS - 1 - p))

        @when(edge & ~odd)
        def _():
            greet(at(2, PANELS - 1 - p))

    @when(core == 1)
    def _():
        greet(at(-1, p))

        @when(odd & (p > 0))
        def _():
            greet(at(-1, p - 1))

        @when(odd & (p < PANELS - 1))
        def _():
            greet(at(-1, p + 1))


    @when(core == 0)
    def _():
        loop(CHUNKS, lambda j: load_chunk(j).wait())
        load_e.wait()

    when(core == 1)(load_o.wait)
    heard = jnp.where(edge & ~odd, jnp.where(core == 0, 2, 4), 3)
    pl.semaphore_wait(barrier, heard + jnp.where((core == 0) & odd, jnp.where(edge, 1, 2), 0))

    @when(core == 0)
    def _():
        @when(odd & (p < PANELS - 1))
        def _():
            loop(EARLY // 2, lambda b: pair_r(p, b, 1).start())

        @when(odd & (p > 0))
        def _():
            loop(EARLY // 2, lambda b: pair_l(p, b, 1).start())

        loop(CHUNKS, lambda j: e_over(j).start())
        acc[...] = jnp.zeros_like(acc)

        @when(edge & odd & (site > 2))
        def _():
            def hand_on(c):
                o_aside(c).wait_recv()
                o_aside_on(c).start()

            loop(BANDS, hand_on)

        def take(i):
            come(i)
            multiply(i)

        def come(i):
            a, j = arrival(i)
            d_over(j).wait_recv()

            @when(passes(a) & ~held(a))
            def _():
                d_pass(j, pass_to(a)).start()

            d_over(j).start()

        def held(a):
            return odd & ~edge & (a == 7)

        def multiply(i):
            _, j = arrival(i)
            columns = pl.ds(pl.multiple_of(j * cols, cols), cols)
            dr, di = drecv[j, 0], drecv[j, 1]
            both = dot(own[0], jnp.concatenate([dr, di], axis=1)) + dot(own[1], jnp.concatenate([-di, dr], axis=1))
            gbuf[0, :, columns] = both[:, :cols].astype(bf16)
            gbuf[1, :, columns] = both[:, cols:].astype(bf16)

        def add(i, final=False):
            _, j = arrival(i)

            def rows_in(n):
                o_copy(j // 2, 2 * lax.rem(j, 2) + n, o_z, at(-3, p), o2buf, o2_recv).wait_recv()

            loop(BANDS // 2, rows_in)
            columns = pl.ds(pl.multiple_of(j * cols, cols), cols)
            gr, gi = gbuf[0, :, columns], gbuf[1, :, columns]
            below = jnp.concatenate([o2buf[0, columns, :], o2buf[1, columns, :]], axis=0)
            re = acc[0] + dot(jnp.concatenate([gr, -gi], axis=1), below)
            im = acc[1] + dot(jnp.concatenate([gi, gr], axis=1), below)
            if final:
                out_ref[0] = re.astype(bf16)
                out_ref[1] = im.astype(bf16)
            else:
                acc[0] = re
                acc[1] = im

        def pair_of(g):
            return jnp.where(low, 2 * g, CHUNKS - 2 - 2 * g)

        def multiply_pair(g):
            j = pair_of(g)
            columns = pl.ds(pl.multiple_of(j * cols, cols), 2 * cols)
            er, ei = own[0], own[1]
            dr = jnp.concatenate([drecv[j, 0], drecv[j + 1, 0]], axis=1)
            di = jnp.concatenate([drecv[j, 1], drecv[j + 1, 1]], axis=1)
            gbuf[0, :, columns] = (dot(er, dr) - dot(ei, di)).astype(bf16)
            gbuf[1, :, columns] = (dot(er, di) + dot(ei, dr)).astype(bf16)

        def add_pair(g, final=False):
            j = pair_of(g)
            loop(BANDS, lambda c: o_copy(j // 2, c, o_z, at(-3, p), o2buf, o2_recv).wait_recv())
            columns = pl.ds(pl.multiple_of(j * cols, cols), 2 * cols)
            gr, gi = gbuf[0, :, columns], gbuf[1, :, columns]
            tr, ti = o2buf[0, columns, :], o2buf[1, columns, :]
            re = acc[0] + (dot(gr, tr) - dot(gi, ti))
            im = acc[1] + (dot(gr, ti) + dot(gi, tr))
            if final:
                out_ref[0] = re.astype(bf16)
                out_ref[1] = im.astype(bf16)
            else:
                acc[0] = re
                acc[1] = im

        def added(i):
            return jnp.where(i < 3, 0, jnp.where(i < 6, 2 * i - 5, i))

        def step(i):
            take(i)

            @when(odd & ~edge & (i == 5))
            def _():
                d_pass(jnp.where(low, 7, 0), pass_to(7)).start()

            def more(n, carry):
                add(n)
                return carry

            @when(site > 1)
            def _():
                lax.fori_loop(added(i - 1), added(i), more, 0)

        def drain(i):
            a, j = arrival(i)
            d_over(j).wait_send()

            @when(passes(a))
            def _():
                d_pass(j, 1).wait_send()

        main = jnp.where(low, 0, 1)
        other = 1 - main

        def span(first, end, f):
            loop(end - first, lambda i: f(first + i))

        def take_rows(k):
            @when(edge)
            def _():
                for g in range(2):
                    rows_pass(main, g, k, 2, pass_to(0)).wait_recv()
                    rows_pass(main, g, k, 2, pass_to(0)).start()

                @when(k > 0)
                def _():
                    rows_pass(other, 0, k - 1, 2, pass_to(0)).wait_recv()

            @when(~edge)
            def _():
                for g in range(2):
                    rows_pass(main, g, k, 2, pass_to(0)).wait_recv()
                    rows_pass(main, g, k, 2 - g, pass_to(0)).start()
                for g in range(2):
                    rows_pass(other, g, k, 2 - g, pass_to(0)).wait_recv()
                    if g == 0:
                        rows_pass(other, g, k, 2, pass_to(7)).start()

        def drain_rows(k):
            rows_pass(main, 0, k, 2, pass_to(0)).wait_send()

            @when(edge)
            def _():
                rows_pass(main, 1, k, 2, pass_to(0)).wait_send()

            @when(~edge)
            def _():
                rows_pass(main, 1, k, 1, pass_to(0)).wait_send()
                rows_pass(other, 0, k, 2, pass_to(7)).wait_send()

        def over(i):
            d_over(arrival(i)[1]).start()

        @when(site == 0)
        def _():
            out_ref[...] = own[...]

        @when((site > 0) & odd)
        def _():
            loop(CHUNKS, step)
            loop(CHUNKS, drain)

        @when((site > 0) & ~odd)
        def _():
            loop(PANELS, take_rows)
            span(0, 4, over)

            @when(~edge)
            def _():
                span(4, 7, over)

            loop(2, multiply_pair)

            @when(edge)
            def _():
                come(4)
                loop(2, add_pair)
                rows_pass(other, 0, PANELS - 1, 2, pass_to(0)).wait_recv()
                span(5, 7, over)

            multiply_pair(3)

            @when(~edge)
            def _():
                come(7)
                loop(2, add_pair)

            add_pair(3)

            @when(edge)
            def _():
                come(7)

            multiply_pair(2)
            add_pair(2, final=True)

        @when(site == 1)
        def _():
            out_ref[...] = gbuf[...]

        @when((site > 1) & odd)
        def _():
            add(CHUNKS - 1, final=True)

        @when((site > 0) & ~odd)
        def _():
            loop(PANELS, drain_rows)
            loop(CHUNKS, lambda j: d_over(j).wait_send())

            @when(edge)
            def _():
                d_pass(arrival(4)[1], 1).wait_send()

        loop(CHUNKS, lambda j: e_over(j).wait_send())

        @when(odd & (p < PANELS - 1))
        def _():
            loop(EARLY // 2, lambda b: pair_r(p, b, 1).wait_send())

        @when(odd & (p > 0))
        def _():
            loop(EARLY // 2, lambda b: pair_l(p, b, 1).wait_send())

        @when(edge & odd & (site > 2))
        def _():
            loop(BANDS, lambda c: o_aside_on(c).wait_send())

    @when(core == 1)
    def _():
        def pass_o(q, c, right, left):
            @when(right & (p < PANELS - 1))
            def _():
                o_r(q, c).start()

            @when(left & (p > 0))
            def _():
                o_l(q, c).start()

            aside = edge & ~odd & (q == p)

            @when((site < sites - 2) & ~aside)
            def _():
                o_up(q, c).start()

            @when((site < sites - 2) & aside)
            def _():
                o_aside(c).start()

        def hop(n):
            def one(c):
                @when(p - 1 - n >= 0)
                def _():
                    o_r(p - 1 - n, c).wait_recv()
                    pass_o(p - 1 - n, c, True, False)

                @when(p + 1 + n < PANELS)
                def _():
                    o_l(p + 1 + n, c).wait_recv()
                    pass_o(p + 1 + n, c, False, True)

            loop(BANDS, one)

        def own_e():
            loop(CHUNKS, lambda j: e_over(j).wait_recv())

        def nth(i):
            return jnp.where(p == 0, CHUNKS - 1 - i, i)

        def product(q, j):
            here = pl.ds(pl.multiple_of(q * rows, rows), rows)
            ar, ai = obuf[0, here, :], obuf[1, here, :]
            br, bi = ebuf[j, 0], ebuf[j, 1]
            re = (dot(ar, br) - dot(ai, bi)).astype(bf16)
            im = (dot(ar, bi) + dot(ai, br)).astype(bf16)
            return re, im

        def two(j, part):
            return jnp.concatenate([ebuf[j, part], ebuf[j + 1, part]], axis=1)

        def rows_of(q, j):
            here = pl.ds(pl.multiple_of(q * rows, rows), rows)
            ar, ai = obuf[0, here, :], obuf[1, here, :]
            br, bi = two(j, 0), two(j, 1)
            re = (dot(ar, br) - dot(ai, bi)).astype(bf16)
            im = (dot(ar, bi) + dot(ai, br)).astype(bf16)
            for n in range(2):
                dsend[j + n, 0, here, :] = re[:, n * cols : (n + 1) * cols]
                dsend[j + n, 1, here, :] = im[:, n * cols : (n + 1) * cols]

        def e_in_chunk(j):
            @when(p == 0)
            def _():
                loop(PANELS - 1, lambda q: e_l(q + 1, j).wait_recv())

            @when(p == 3)
            def _():
                loop(PANELS - 1, lambda q: e_r(q, j).wait_recv())

        def copy_own(j):
            mine = pl.ds(pl.multiple_of(p * rows, rows), rows)
            dloc[:, :, pl.ds(pl.multiple_of(j * cols, cols), cols)] = dsend[j, :, mine, :]

        def own_chunk(j):
            columns = pl.ds(pl.multiple_of(j * cols, cols), cols)
            re, im = product(p, j)
            dloc[0, :, columns] = re
            dloc[1, :, columns] = im

        def whole_chunk(i):
            j = nth(i)
            e_in_chunk(j)

            def block(q):
                here = pl.ds(pl.multiple_of(q * rows, rows), rows)
                both = (dot(obuf[0, here, :], wide[0]) + dot(obuf[1, here, :], wide[1])).astype(bf16)
                dsend[j, 0, here, :] = both[:, :cols]
                dsend[j, 1, here, :] = both[:, cols:]

            @when(i < direct_out)
            def _():
                wide[0] = jnp.concatenate([ebuf[j, 0], ebuf[j, 1]], axis=1)
                wide[1] = jnp.concatenate([-ebuf[j, 1], ebuf[j, 0]], axis=1)
                loop(PANELS, block)

                @when(site < sites - 1)
                def _():
                    d_next(j).start()

                copy_own(j)

            @when(i >= direct_out)
            def _():
                own_chunk(j)

        @when(~odd)
        def _():
            loop(BANDS, lambda c: pass_o(p, c, True, True))
            hop(0)
            own_e()

            @when(p == 0)
            def _():
                loop(CHUNKS, lambda j: e_r(0, j).start())

            @when(p == 3)
            def _():
                loop(CHUNKS, lambda j: e_l(3, CHUNKS - 1 - j).start())

            hop(1)

            @when(p == 1)
            def _():
                def one(j):
                    e_r(1, j).start()
                    e_r(0, j).wait_recv()
                    e_r(0, j).start()

                loop(CHUNKS, one)

            @when(p == 2)
            def _():
                def one(i):
                    j = CHUNKS - 1 - i
                    e_l(2, j).start()
                    e_l(3, j).wait_recv()
                    e_l(3, j).start()

                loop(CHUNKS, one)

            hop(2)

            @when(p == 1)
            def _():
                def one(i):
                    j = CHUNKS - 1 - i
                    e_l(1, j).start()
                    e_l(2, j).wait_recv()
                    e_l(2, j).start()
                    e_l(3, j).wait_recv()
                    e_l(3, j).start()

                loop(CHUNKS, one)

            @when(p == 2)
            def _():
                def one(j):
                    e_r(2, j).start()
                    e_r(1, j).wait_recv()
                    e_r(1, j).start()
                    e_r(0, j).wait_recv()
                    e_r(0, j).start()

                loop(CHUNKS, one)

            @when(edge)
            def _():
                loop(CHUNKS, whole_chunk)

        sent = jnp.where(p == 0, 1, 0)

        @when(odd)
        def _():
            def pass_e(q, b, right, left):
                @when(right & (p < PANELS - 1))
                def _():
                    pair_r(q, b).start()

                @when(left & (p > 0))
                def _():
                    pair_l(q, b).start()

            def own_o(n):
                def one(c):
                    @when((p == n) & (p < PANELS - 1))
                    def _():
                        o_r(p, c).start()

                    @when((p == PANELS - 1 - n) & (p > 0))
                    def _():
                        o_l(p, c).start()

                loop(BANDS, one)

            @when(site < sites - 2)
            def _():
                loop(BANDS, lambda c: o_up(p, c).start())

            for n in range(PANELS - 1):
                def one(b):
                    @when(p - 1 - n >= 0)
                    def _():
                        pair_r(p - 1 - n, b).wait_recv()
                        pass_e(p - 1 - n, b, True, False)

                    @when(p + 1 + n < PANELS)
                    def _():
                        pair_l(p + 1 + n, b).wait_recv()
                        pass_e(p + 1 + n, b, False, True)

                loop(EARLY // 2, one)
                if n == 0:
                    own_o(0)
                own_o(n + 1)

            def send_rows(k):
                @when(edge)
                def _():
                    for g in range(2):
                        rows_of(jnp.where(p == 0, k, PANELS - 1 - k), jnp.where(p == 0, CHUNKS - 2 - 2 * g, 2 * g))

                        @when(site < sites - 1)
                        def _():
                            rows_next(sent, g, k).start()

            own_e()
            send_rows(0)
            hop(0)
            send_rows(1)

            @when(p == 0)
            def _():
                loop(EARLY, lambda i: e_r(0, EARLY + i).start())

            @when(p == 3)
            def _():
                loop(EARLY, lambda i: e_l(3, EARLY - 1 - i).start())

            hop(1)
            send_rows(2)

            @when(p == 1)
            def _():
                def one(i):
                    j = EARLY + i
                    e_r(1, j).start()
                    e_r(0, j).wait_recv()
                    e_r(0, j).start()

                loop(EARLY, one)

            @when(p == 2)
            def _():
                def one(i):
                    j = EARLY - 1 - i
                    e_l(2, j).start()
                    e_l(3, j).wait_recv()
                    e_l(3, j).start()

                loop(EARLY, one)

            hop(2)
            send_rows(3)

            @when(p == 1)
            def _():
                def one(i):
                    j = EARLY - 1 - i
                    e_l(1, j).start()
                    e_l(2, j).wait_recv()
                    e_l(2, j).start()
                    e_l(3, j).wait_recv()
                    e_l(3, j).start()

                loop(EARLY, one)

            @when(p == 2)
            def _():
                def one(i):
                    j = EARLY + i
                    e_r(2, j).start()
                    e_r(1, j).wait_recv()
                    e_r(1, j).start()
                    e_r(0, j).wait_recv()
                    e_r(0, j).start()

                loop(EARLY, one)

            @when(edge)
            def _():
                loop(EARLY, lambda i: whole_chunk(EARLY + i))
                loop(EARLY, lambda i: copy_own(nth(i)))

        @when(~edge)
        def _():
            loop(CHUNKS, own_chunk)

        def step(i):
            _, j = arrival(i)
            d_over(j).wait_recv()
            columns = pl.ds(pl.multiple_of(j * cols, cols), cols)
            br, bi = drecv[j, 0], drecv[j, 1]
            both = dot(dloc[0], jnp.concatenate([br, bi], axis=1)) + dot(dloc[1], jnp.concatenate([-bi, br], axis=1))
            re, im = both[:, :cols].astype(bf16), both[:, cols:].astype(bf16)
            out_ref[0, :, columns] = re
            out_ref[1, :, columns] = im

        @when(site == 0)
        def _():
            out_ref[...] = dloc[...]

        def step_pair(i):
            g = pick(i, (0, 1, 3, 2))
            j = jnp.where(low, 2 * g, CHUNKS - 2 - 2 * g)
            loop(2, lambda n: d_over(j + n).wait_recv())
            columns = pl.ds(pl.multiple_of(j * cols, cols), 2 * cols)
            ar, ai = dloc[0], dloc[1]
            br = jnp.concatenate([drecv[j, 0], drecv[j + 1, 0]], axis=1)
            bi = jnp.concatenate([drecv[j, 1], drecv[j + 1, 1]], axis=1)
            out_ref[0, :, columns] = (dot(ar, br) - dot(ai, bi)).astype(bf16)
            out_ref[1, :, columns] = (dot(ar, bi) + dot(ai, br)).astype(bf16)

        @when((site > 0) & ~odd)
        def _():
            loop(CHUNKS // 2, step_pair)

        @when((site > 0) & odd)
        def _():
            loop(CHUNKS, step)

        def drain_o(i):
            q, c = i // BANDS, lax.rem(i, BANDS)

            @when(site < sites - 2)
            def _():
                o_up(q, c).wait_send()

            @when((q <= p) & (p < PANELS - 1))
            def _():
                o_r(q, c).wait_send()

            @when((q >= p) & (p > 0))
            def _():
                o_l(q, c).wait_send()

        loop(PANELS * BANDS, drain_o)

        def drain_e(i):
            q, j = i // CHUNKS, lax.rem(i, CHUNKS)

            @when((q <= p) & (p < PANELS - 1))
            def _():
                @when(~odd | (j >= EARLY))
                def _():
                    e_r(q, j).wait_send()

                @when(odd & (q < p) & (j < EARLY // 2))
                def _():
                    pair_r(q, j).wait_send()

            @when((q >= p) & (p > 0))
            def _():
                @when(~odd | (j < EARLY))
                def _():
                    e_l(q, j).wait_send()

                @when(odd & (q > p) & (j >= EARLY) & (j < EARLY + EARLY // 2))
                def _():
                    pair_l(q, j - EARLY).wait_send()

        loop(PANELS * CHUNKS, drain_e)

        @when(edge)
        def _():
            def drain_d(i):
                @when((i < direct_out) & (site < sites - 1) & (~odd | (i >= EARLY)))
                def _():
                    d_next(nth(i)).wait_send()

            loop(CHUNKS, drain_d)

            @when(odd & (site < sites - 1))
            def _():
                for g in range(2):
                    loop(PANELS, lambda k: rows_next(sent, g, k).wait_send())


def shards(forward_props):
    x = forward_props[:, 0]
    _, rows, width = x.shape
    cols = width // CHUNKS
    dma = pltpu.SemaphoreType.DMA
    tm_size = lax.axis_size("tm")
    out = pl.pallas_call(
        functools.partial(kernel, tm_size),
        out_shape=jax.ShapeDtypeStruct(x.shape, bf16),
        in_specs=[pl.BlockSpec(memory_space=pl.ANY)],
        out_specs=pl.BlockSpec(memory_space=pltpu.VMEM),
        scratch_shapes=[
            pltpu.VMEM(x.shape, bf16),
            pltpu.VMEM((2, width, width), bf16),
            pltpu.VMEM((2, width, width), bf16),
            pltpu.VMEM((CHUNKS, 2, width, cols), bf16),
            pltpu.VMEM((CHUNKS, 2, width, cols), bf16),
            pltpu.VMEM((CHUNKS, 2, width, cols), bf16),
            pltpu.VMEM(x.shape, bf16),
            pltpu.VMEM(x.shape, bf16),
            pltpu.VMEM(x.shape, f32),
            dma((CHUNKS + 1,)),
            dma((PANELS, BANDS)),
            dma((PANELS, BANDS)),
            dma((PANELS, BANDS)),
            dma((PANELS, BANDS)),
            dma((PANELS, BANDS)),
            dma((PANELS, CHUNKS)),
            dma((PANELS, CHUNKS)),
            dma((PANELS, CHUNKS)),
            dma((CHUNKS,)),
            dma((CHUNKS,)),
            dma((CHUNKS,)),
            dma((CHUNKS,)),
            pltpu.VMEM(x.shape, bf16),
            dma((BANDS,)),
            dma((BANDS,)),
            dma((2, 2 * PANELS)),
            dma((2, 2 * PANELS)),
            pltpu.VMEM((2, width, 2 * cols), bf16),
        ],
        compiler_params=pltpu.CompilerParams(
            collective_id=0, has_side_effects=True, vmem_limit_bytes=52 * 2**20
        ),
        name="prefix_products",
    )(x)
    return out[:, None]


def solution(mesh):
    placed = (P(None, "tm", "panel", None),)
    return jax.shard_map(
        shards, mesh=mesh, in_specs=placed, out_specs=P(None, "tm", "panel", None), check_vma=False
    )
```

```python
import functools

import jax
import jax.numpy as jnp
from jax import lax
from jax.experimental import pallas as pl
from jax.experimental.pallas import tpu as pltpu
from jax.sharding import PartitionSpec as P

PANELS = 4
CHUNKS = 8
HELD = 2
EARLY = 4
BANDS = 4

bf16, f32 = jnp.bfloat16, jnp.float32


def dot(a, b):
    return jnp.dot(a, b, preferred_element_type=f32)


def when(cond):
    return pl.when(cond)


def loop(n, body):
    def step(i, carry):
        body(i)
        return carry

    lax.fori_loop(0, n, step, 0)


def kernel(
    tm_size, x_ref, out_ref, own, obuf, o2buf, ebuf, dsend, drecv, dloc, gbuf, acc,
    in_sem, o_recv, o_right, o_left, o_z, o2_recv, e_recv, e_right, e_left, e_in, d_recv, d_out, d_in,
    relay, relay_recv, relay_out, rows_recv, rows_out, wide,
):
    rows, width = x_ref.shape[1], x_ref.shape[2]
    cols = width // CHUNKS
    band = rows // BANDS
    tm, p = lax.axis_index("tm"), lax.axis_index("panel")
    core = lax.rem(tm, 2)
    site, sites = tm // 2, tm_size // 2

    def at(shift, panel):
        return (lax.rem(tm + shift + tm_size, tm_size), panel)

    def remote(src, dst, send, recv, where):
        return pltpu.make_async_remote_copy(
            src_ref=src, dst_ref=dst, send_sem=send, recv_sem=recv,
            device_id=where, device_id_type=pl.DeviceIdType.MESH,
        )

    def o_rows(q, c):
        return pl.ds(pl.multiple_of(q * rows + c * band, band), band)

    def o_copy(q, c, sems, where, dst=None, recv=None):
        piece = obuf.at[:, o_rows(q, c), :]
        target = piece if dst is None else dst.at[:, o_rows(q, c), :]
        arrive = (o_recv if recv is None else recv).at[q, c]
        return remote(piece, target, sems.at[q, c], arrive, where)

    def o_r(q, c):
        return o_copy(q, c, o_right, at(0, lax.rem(p + 1, PANELS)))

    def o_l(q, c):
        return o_copy(q, c, o_left, at(0, lax.rem(p + PANELS - 1, PANELS)))

    def o_up(q, c):
        return o_copy(q, c, o_z, at(3, p), o2buf, o2_recv)

    def o_aside(c):
        here = pl.ds(pl.multiple_of(c * band, band), band)
        return remote(
            obuf.at[:, o_rows(p, c), :], relay.at[:, here, :], o_z.at[p, c], relay_recv.at[c], at(5, PANELS - 1 - p)
        )

    def o_aside_on(c):
        here = pl.ds(pl.multiple_of(c * band, band), band)
        q = PANELS - 1 - p
        return remote(relay.at[:, here, :], o2buf.at[:, o_rows(q, c), :], relay_out.at[c], o2_recv.at[q, c], at(-2, q))

    def e_piece(q, j):
        return ebuf.at[j, :, pl.ds(pl.multiple_of(q * rows, rows), rows), :]

    def e_copy(q, j, sems, panel):
        return remote(e_piece(q, j), e_piece(q, j), sems.at[q, j], e_recv.at[q, j], at(0, panel))

    def e_r(q, j):
        return e_copy(q, j, e_right, lax.rem(p + 1, PANELS))

    def e_l(q, j):
        return e_copy(q, j, e_left, lax.rem(p + PANELS - 1, PANELS))

    def e_over(j):
        return remote(e_piece(p, j), e_piece(p, j), e_in.at[j], e_recv.at[p, j], at(1, p))

    def pair(q, j, sems, shift, panel):
        view = ebuf.at[pl.ds(j, 2), :, pl.ds(pl.multiple_of(q * rows, rows), rows), :]
        return remote(view, view, sems.at[q, j], e_recv.at[q, j], at(shift, panel))

    def pair_r(q, b, shift=0):
        return pair(q, 2 * b, e_right, shift, lax.rem(p + 1, PANELS))

    def pair_l(q, b, shift=0):
        return pair(q, CHUNKS - 2 - 2 * b, e_left, shift, lax.rem(p + PANELS - 1, PANELS))

    def d_next(j):
        return remote(dsend.at[j], drecv.at[j], d_out.at[j], d_recv.at[j], at(1, PANELS - 1 - p))

    def d_pass(j, panel):
        return remote(drecv.at[j], drecv.at[j], d_out.at[j], d_recv.at[j], at(0, panel))

    def d_over(j):
        return remote(drecv.at[j], drecv.at[j], d_in.at[j], d_recv.at[j], at(1, p))

    def piece(half, g, k, n):
        first = 2 * g
        q = jnp.where(half == 0, PANELS - 1 - k, k)
        j = jnp.where(half == 0, first, CHUNKS - first - n)
        return pl.ds(j, n), slice(None), pl.ds(pl.multiple_of(q * rows, rows), rows), slice(None)

    def rows_next(half, g, k):
        view = piece(half, g, k, 2)
        m = PANELS * g + k
        return remote(
            dsend.at[view], drecv.at[view], rows_out.at[half, m], rows_recv.at[half, m], at(1, PANELS - 1 - p)
        )

    def rows_pass(half, g, k, n, panel):
        view = piece(half, g, k, n)
        m = PANELS * g + k
        return remote(drecv.at[view], drecv.at[view], rows_out.at[half, m], rows_recv.at[half, m], at(0, panel))

    odd = lax.rem(site, 2) == 1
    direct_out = jnp.where(odd, 6, 7)
    direct_in = jnp.where(odd, 7, 6)
    edge = (p == 0) | (p == PANELS - 1)
    low = p < PANELS // 2

    def pick(i, values):
        found = values[-1]
        for n in range(len(values) - 1):
            found = jnp.where(i == n, values[n], found)
        return found

    def arrival(i):
        inner = jnp.where(odd, pick(i, (0, 1, 7, 2, 6, 3, 5, 4)), pick(i, (0, 1, 2, 3, 7, 6, 5, 4)))
        outer = pick(i, (0, 1, 2, 3, 4, 7, 6, 5))
        a = jnp.where(edge, outer, inner)
        j = jnp.where(low, a, CHUNKS - 1 - a)
        return a, j

    def passes(a):
        return jnp.where(edge, a < 5, (a < 3) | (a >= direct_in))

    def pass_to(a):
        onward = jnp.where(edge, jnp.where(low, 1, 2), jnp.where(low, 2, 1))
        back = jnp.where(low, 0, PANELS - 1)
        return jnp.where(~edge & (a >= direct_in), back, onward)

    def load_chunk(j):
        columns = pl.ds(pl.multiple_of(j * cols, cols), cols)
        return pltpu.make_async_copy(x_ref.at[:, :, columns], e_piece(p, j), in_sem.at[j])

    load_e = pltpu.make_async_copy(x_ref, own, in_sem.at[CHUNKS])
    load_o = pltpu.make_async_copy(
        x_ref, obuf.at[:, pl.ds(pl.multiple_of(p * rows, rows), rows), :], in_sem.at[CHUNKS]
    )

    @when(core == 0)
    def _():
        loop(CHUNKS, lambda j: load_chunk(j).start())
        load_e.start()

    when(core == 1)(load_o.start)

    barrier = pltpu.get_barrier_semaphore()

    def greet(where):
        pl.semaphore_signal(barrier, inc=1, device_id=where, device_id_type=pl.DeviceIdType.MESH)

    @when(p > 0)
    def _():
        greet(at(0, p - 1))

    @when(p < PANELS - 1)
    def _():
        greet(at(0, p + 1))

    @when(core == 0)
    def _():
        greet(at(-3, p))

        @when(edge)
        def _():
            greet(at(-1, PANELS - 1 - p))

        @when(edge & odd)
        def _():
            greet(at(-5, PANELS - 1 - p))

        @when(edge & ~odd)
        def _():
            greet(at(2, PANELS - 1 - p))

    @when(core == 1)
    def _():
        greet(at(-1, p))

        @when(odd & (p > 0))
        def _():
            greet(at(-1, p - 1))

        @when(odd & (p < PANELS - 1))
        def _():
            greet(at(-1, p + 1))


    @when(core == 0)
    def _():
        loop(CHUNKS, lambda j: load_chunk(j).wait())

    when(core == 1)(load_o.wait)
    heard = jnp.where(edge & ~odd, jnp.where(core == 0, 2, 4), 3)
    pl.semaphore_wait(barrier, heard + jnp.where((core == 0) & odd, jnp.where(edge, 1, 2), 0))

    @when(core == 0)
    def _():
        @when(odd & (p < PANELS - 1))
        def _():
            loop(EARLY // 2, lambda b: pair_r(p, b, 1).start())

        @when(odd & (p > 0))
        def _():
            loop(EARLY // 2, lambda b: pair_l(p, b, 1).start())

        loop(CHUNKS, lambda j: e_over(j).start())
        load_e.wait()
        acc[...] = jnp.zeros_like(acc)

        @when(edge & odd & (site > 2))
        def _():
            def hand_on(c):
                o_aside(c).wait_recv()
                o_aside_on(c).start()

            loop(BANDS, hand_on)

        def take(i):
            come(i)
            multiply(i)

        def come(i):
            a, j = arrival(i)
            d_over(j).wait_recv()

            @when(passes(a) & ~held(a))
            def _():
                d_pass(j, pass_to(a)).start()

            d_over(j).start()

        def held(a):
            return odd & ~edge & (a == 7)

        def multiply(i):
            _, j = arrival(i)
            columns = pl.ds(pl.multiple_of(j * cols, cols), cols)
            dr, di = drecv[j, 0], drecv[j, 1]
            both = dot(own[0], jnp.concatenate([dr, di], axis=1)) + dot(own[1], jnp.concatenate([-di, dr], axis=1))
            gbuf[0, :, columns] = both[:, :cols].astype(bf16)
            gbuf[1, :, columns] = both[:, cols:].astype(bf16)

        def add(i, final=False):
            _, j = arrival(i)

            def rows_in(n):
                o_copy(j // 2, 2 * lax.rem(j, 2) + n, o_z, at(-3, p), o2buf, o2_recv).wait_recv()

            loop(BANDS // 2, rows_in)
            columns = pl.ds(pl.multiple_of(j * cols, cols), cols)
            gr, gi = gbuf[0, :, columns], gbuf[1, :, columns]
            below = jnp.concatenate([o2buf[0, columns, :], o2buf[1, columns, :]], axis=0)
            re = acc[0] + dot(jnp.concatenate([gr, -gi], axis=1), below)
            im = acc[1] + dot(jnp.concatenate([gi, gr], axis=1), below)
            if final:
                out_ref[0] = re.astype(bf16)
                out_ref[1] = im.astype(bf16)
            else:
                acc[0] = re
                acc[1] = im

        def pair_of(g):
            return jnp.where(low, 2 * g, CHUNKS - 2 - 2 * g)

        def multiply_pair(g):
            j = pair_of(g)
            columns = pl.ds(pl.multiple_of(j * cols, cols), 2 * cols)
            er, ei = own[0], own[1]
            dr = jnp.concatenate([drecv[j, 0], drecv[j + 1, 0]], axis=1)
            di = jnp.concatenate([drecv[j, 1], drecv[j + 1, 1]], axis=1)
            gbuf[0, :, columns] = (dot(er, dr) - dot(ei, di)).astype(bf16)
            gbuf[1, :, columns] = (dot(er, di) + dot(ei, dr)).astype(bf16)

        def add_pair(g, final=False):
            j = pair_of(g)
            loop(BANDS, lambda c: o_copy(j // 2, c, o_z, at(-3, p), o2buf, o2_recv).wait_recv())
            columns = pl.ds(pl.multiple_of(j * cols, cols), 2 * cols)
            gr, gi = gbuf[0, :, columns], gbuf[1, :, columns]
            tr, ti = o2buf[0, columns, :], o2buf[1, columns, :]
            re = acc[0] + (dot(gr, tr) - dot(gi, ti))
            im = acc[1] + (dot(gr, ti) + dot(gi, tr))
            if final:
                out_ref[0] = re.astype(bf16)
                out_ref[1] = im.astype(bf16)
            else:
                acc[0] = re
                acc[1] = im

        def added(i):
            return jnp.where(i < 3, 0, jnp.where(i < 6, 2 * i - 5, i))

        def step(i):
            take(i)

            @when(odd & ~edge & (i == 5))
            def _():
                d_pass(jnp.where(low, 7, 0), pass_to(7)).start()

            def more(n, carry):
                add(n)
                return carry

            @when(site > 1)
            def _():
                lax.fori_loop(added(i - 1), added(i), more, 0)

        def drain(i):
            a, j = arrival(i)
            d_over(j).wait_send()

            @when(passes(a))
            def _():
                d_pass(j, 1).wait_send()

        main = jnp.where(low, 0, 1)
        other = 1 - main

        def span(first, end, f):
            loop(end - first, lambda i: f(first + i))

        def give_back(k):
            def one(n, carry):
                rows_pass(other, 0, n, 2, pass_to(7)).start()
                return carry

            lax.fori_loop(jnp.where(k == HELD, 0, k), jnp.where(k < HELD, k, k + 1), one, 0)

        def take_rows(k):
            @when(edge)
            def _():
                for g in range(2):
                    rows_pass(main, g, k, 2, pass_to(0)).wait_recv()
                    rows_pass(main, g, k, 2, pass_to(0)).start()

            @when(~edge)
            def _():
                for g in range(2):
                    rows_pass(main, g, k, 2, pass_to(0)).wait_recv()
                    rows_pass(main, g, k, 2 - g, pass_to(0)).start()
                for g in range(2):
                    rows_pass(other, g, k, 2 - g, pass_to(0)).wait_recv()
                    if g == 0:
                        give_back(k)

        def drain_rows(k):
            rows_pass(main, 0, k, 2, pass_to(0)).wait_send()

            @when(edge)
            def _():
                rows_pass(main, 1, k, 2, pass_to(0)).wait_send()

            @when(~edge)
            def _():
                rows_pass(main, 1, k, 1, pass_to(0)).wait_send()
                rows_pass(other, 0, k, 2, pass_to(7)).wait_send()

        def over(i):
            d_over(arrival(i)[1]).start()

        loop(CHUNKS, lambda j: e_over(j).wait_send())

        @when(odd & (p < PANELS - 1))
        def _():
            loop(EARLY // 2, lambda b: pair_r(p, b, 1).wait_send())

        @when(odd & (p > 0))
        def _():
            loop(EARLY // 2, lambda b: pair_l(p, b, 1).wait_send())

        @when(edge & odd & (site > 2))
        def _():
            loop(BANDS, lambda c: o_aside_on(c).wait_send())

        @when(site == 0)
        def _():
            out_ref[...] = own[...]

        @when((site > 0) & odd)
        def _():
            loop(CHUNKS, step)
            loop(CHUNKS, drain)

        @when((site > 0) & ~odd)
        def _():
            loop(PANELS, take_rows)
            span(0, 4, over)

            @when(~edge)
            def _():
                span(4, 7, over)

            loop(2, multiply_pair)

            @when(edge)
            def _():
                come(4)
                loop(2, add_pair)
                loop(PANELS, lambda k: rows_pass(other, 0, k, 2, pass_to(0)).wait_recv())
                span(5, 7, over)
                come(7)

            multiply_pair(3)

            @when(~edge)
            def _():
                loop(2, add_pair)

            add_pair(3)

            @when(~edge)
            def _():
                come(7)

            loop(PANELS, drain_rows)
            multiply_pair(2)
            add_pair(2, final=True)

        @when(site == 1)
        def _():
            out_ref[...] = gbuf[...]

        @when((site > 1) & odd)
        def _():
            add(CHUNKS - 1, final=True)

        @when((site > 0) & ~odd)
        def _():
            loop(CHUNKS, lambda j: d_over(j).wait_send())

            @when(edge)
            def _():
                d_pass(arrival(4)[1], 1).wait_send()

    @when(core == 1)
    def _():
        def pass_o(q, c, right, left):
            @when(right & (p < PANELS - 1))
            def _():
                o_r(q, c).start()

            @when(left & (p > 0))
            def _():
                o_l(q, c).start()

            aside = edge & ~odd & (q == p)

            @when((site < sites - 2) & ~aside)
            def _():
                o_up(q, c).start()

            @when((site < sites - 2) & aside)
            def _():
                o_aside(c).start()

        def hop(n):
            def one(c):
                @when(p - 1 - n >= 0)
                def _():
                    o_r(p - 1 - n, c).wait_recv()
                    pass_o(p - 1 - n, c, True, False)

                @when(p + 1 + n < PANELS)
                def _():
                    o_l(p + 1 + n, c).wait_recv()
                    pass_o(p + 1 + n, c, False, True)

            loop(BANDS, one)

        def own_e():
            loop(CHUNKS, lambda j: e_over(j).wait_recv())

        def nth(i):
            return jnp.where(p == 0, CHUNKS - 1 - i, i)

        def product(q, j):
            here = pl.ds(pl.multiple_of(q * rows, rows), rows)
            ar, ai = obuf[0, here, :], obuf[1, here, :]
            br, bi = ebuf[j, 0], ebuf[j, 1]
            re = (dot(ar, br) - dot(ai, bi)).astype(bf16)
            im = (dot(ar, bi) + dot(ai, br)).astype(bf16)
            return re, im

        def two(j, part):
            return jnp.concatenate([ebuf[j, part], ebuf[j + 1, part]], axis=1)

        def rows_of(q, j):
            here = pl.ds(pl.multiple_of(q * rows, rows), rows)
            ar, ai = obuf[0, here, :], obuf[1, here, :]
            br, bi = two(j, 0), two(j, 1)
            re = (dot(ar, br) - dot(ai, bi)).astype(bf16)
            im = (dot(ar, bi) + dot(ai, br)).astype(bf16)
            for n in range(2):
                dsend[j + n, 0, here, :] = re[:, n * cols : (n + 1) * cols]
                dsend[j + n, 1, here, :] = im[:, n * cols : (n + 1) * cols]

        def e_in_chunk(j):
            @when(p == 0)
            def _():
                loop(PANELS - 1, lambda q: e_l(q + 1, j).wait_recv())

            @when(p == 3)
            def _():
                loop(PANELS - 1, lambda q: e_r(q, j).wait_recv())

        def copy_own(j):
            mine = pl.ds(pl.multiple_of(p * rows, rows), rows)
            dloc[:, :, pl.ds(pl.multiple_of(j * cols, cols), cols)] = dsend[j, :, mine, :]

        def own_chunk(j):
            columns = pl.ds(pl.multiple_of(j * cols, cols), cols)
            re, im = product(p, j)
            dloc[0, :, columns] = re
            dloc[1, :, columns] = im

        def whole_chunk(i):
            j = nth(i)
            e_in_chunk(j)

            def block(q):
                here = pl.ds(pl.multiple_of(q * rows, rows), rows)
                both = (dot(obuf[0, here, :], wide[0]) + dot(obuf[1, here, :], wide[1])).astype(bf16)
                dsend[j, 0, here, :] = both[:, :cols]
                dsend[j, 1, here, :] = both[:, cols:]

            @when(i < direct_out)
            def _():
                wide[0] = jnp.concatenate([ebuf[j, 0], ebuf[j, 1]], axis=1)
                wide[1] = jnp.concatenate([-ebuf[j, 1], ebuf[j, 0]], axis=1)
                loop(PANELS, block)

                @when(site < sites - 1)
                def _():
                    d_next(j).start()

                copy_own(j)

            @when(i >= direct_out)
            def _():
                own_chunk(j)

        @when(~odd)
        def _():
            loop(BANDS, lambda c: pass_o(p, c, True, True))
            hop(0)
            own_e()

            @when(p == 0)
            def _():
                loop(CHUNKS, lambda j: e_r(0, j).start())

            @when(p == 3)
            def _():
                loop(CHUNKS, lambda j: e_l(3, CHUNKS - 1 - j).start())

            hop(1)

            @when(p == 1)
            def _():
                def one(j):
                    e_r(1, j).start()
                    e_r(0, j).wait_recv()
                    e_r(0, j).start()

                loop(CHUNKS, one)

            @when(p == 2)
            def _():
                def one(i):
                    j = CHUNKS - 1 - i
                    e_l(2, j).start()
                    e_l(3, j).wait_recv()
                    e_l(3, j).start()

                loop(CHUNKS, one)

            hop(2)

            @when(p == 1)
            def _():
                def one(i):
                    j = CHUNKS - 1 - i
                    e_l(1, j).start()
                    e_l(2, j).wait_recv()
                    e_l(2, j).start()
                    e_l(3, j).wait_recv()
                    e_l(3, j).start()

                loop(CHUNKS, one)

            @when(p == 2)
            def _():
                def one(j):
                    e_r(2, j).start()
                    e_r(1, j).wait_recv()
                    e_r(1, j).start()
                    e_r(0, j).wait_recv()
                    e_r(0, j).start()

                loop(CHUNKS, one)

            @when(edge)
            def _():
                loop(CHUNKS, whole_chunk)

        sent = jnp.where(p == 0, 1, 0)

        @when(odd)
        def _():
            def pass_e(q, b, right, left):
                @when(right & (p < PANELS - 1))
                def _():
                    pair_r(q, b).start()

                @when(left & (p > 0))
                def _():
                    pair_l(q, b).start()

            def own_o(n):
                def one(c):
                    @when((p == n) & (p < PANELS - 1))
                    def _():
                        o_r(p, c).start()

                    @when((p == PANELS - 1 - n) & (p > 0))
                    def _():
                        o_l(p, c).start()

                loop(BANDS, one)

            @when(site < sites - 2)
            def _():
                loop(BANDS, lambda c: o_up(p, c).start())

            for n in range(PANELS - 1):
                def one(b):
                    @when(p - 1 - n >= 0)
                    def _():
                        pair_r(p - 1 - n, b).wait_recv()
                        pass_e(p - 1 - n, b, True, False)

                    @when(p + 1 + n < PANELS)
                    def _():
                        pair_l(p + 1 + n, b).wait_recv()
                        pass_e(p + 1 + n, b, False, True)

                loop(EARLY // 2, one)
                if n == 0:
                    own_o(0)
                own_o(n + 1)

            def send_rows(k):
                @when(edge)
                def _():
                    for g in range(2):
                        rows_of(jnp.where(p == 0, k, PANELS - 1 - k), jnp.where(p == 0, CHUNKS - 2 - 2 * g, 2 * g))

                        @when(site < sites - 1)
                        def _():
                            rows_next(sent, g, k).start()

            own_e()
            send_rows(0)
            hop(0)
            send_rows(1)

            @when(p == 0)
            def _():
                loop(EARLY, lambda i: e_r(0, EARLY + i).start())

            @when(p == 3)
            def _():
                loop(EARLY, lambda i: e_l(3, EARLY - 1 - i).start())

            hop(1)
            send_rows(2)

            @when(p == 1)
            def _():
                def one(i):
                    j = EARLY + i
                    e_r(1, j).start()
                    e_r(0, j).wait_recv()
                    e_r(0, j).start()

                loop(EARLY, one)

            @when(p == 2)
            def _():
                def one(i):
                    j = EARLY - 1 - i
                    e_l(2, j).start()
                    e_l(3, j).wait_recv()
                    e_l(3, j).start()

                loop(EARLY, one)

            hop(2)
            send_rows(3)

            @when(p == 1)
            def _():
                def one(i):
                    j = EARLY - 1 - i
                    e_l(1, j).start()
                    e_l(2, j).wait_recv()
                    e_l(2, j).start()
                    e_l(3, j).wait_recv()
                    e_l(3, j).start()

                loop(EARLY, one)

            @when(p == 2)
            def _():
                def one(i):
                    j = EARLY + i
                    e_r(2, j).start()
                    e_r(1, j).wait_recv()
                    e_r(1, j).start()
                    e_r(0, j).wait_recv()
                    e_r(0, j).start()

                loop(EARLY, one)

            @when(edge)
            def _():
                loop(EARLY, lambda i: whole_chunk(EARLY + i))
                loop(EARLY, lambda i: copy_own(nth(i)))

        @when(~edge)
        def _():
            loop(CHUNKS, own_chunk)

        def drain_o(i):
            q, c = i // BANDS, lax.rem(i, BANDS)

            @when(site < sites - 2)
            def _():
                o_up(q, c).wait_send()

            @when((q <= p) & (p < PANELS - 1))
            def _():
                o_r(q, c).wait_send()

            @when((q >= p) & (p > 0))
            def _():
                o_l(q, c).wait_send()

        loop(PANELS * BANDS, drain_o)

        def drain_e(i):
            q, j = i // CHUNKS, lax.rem(i, CHUNKS)

            @when((q <= p) & (p < PANELS - 1))
            def _():
                @when(~odd | (j >= EARLY))
                def _():
                    e_r(q, j).wait_send()

                @when(odd & (q < p) & (j < EARLY // 2))
                def _():
                    pair_r(q, j).wait_send()

            @when((q >= p) & (p > 0))
            def _():
                @when(~odd | (j < EARLY))
                def _():
                    e_l(q, j).wait_send()

                @when(odd & (q > p) & (j >= EARLY) & (j < EARLY + EARLY // 2))
                def _():
                    pair_l(q, j - EARLY).wait_send()

        loop(PANELS * CHUNKS, drain_e)

        def step(i):
            _, j = arrival(i)
            d_over(j).wait_recv()
            columns = pl.ds(pl.multiple_of(j * cols, cols), cols)
            br, bi = drecv[j, 0], drecv[j, 1]
            both = dot(dloc[0], jnp.concatenate([br, bi], axis=1)) + dot(dloc[1], jnp.concatenate([-bi, br], axis=1))
            re, im = both[:, :cols].astype(bf16), both[:, cols:].astype(bf16)
            out_ref[0, :, columns] = re
            out_ref[1, :, columns] = im

        def drain_sent():
            def drain_d(i):
                @when((i < direct_out) & (site < sites - 1) & (~odd | (i >= EARLY)))
                def _():
                    d_next(nth(i)).wait_send()

            loop(CHUNKS, drain_d)

            @when(odd & (site < sites - 1))
            def _():
                for g in range(2):
                    loop(PANELS, lambda k: rows_next(sent, g, k).wait_send())

        when(edge & odd)(drain_sent)

        @when(site == 0)
        def _():
            out_ref[...] = dloc[...]

        def step_pair(i):
            g = pick(i, (0, 1, 3, 2))
            j = jnp.where(low, 2 * g, CHUNKS - 2 - 2 * g)
            loop(2, lambda n: d_over(j + n).wait_recv())
            columns = pl.ds(pl.multiple_of(j * cols, cols), 2 * cols)
            ar, ai = dloc[0], dloc[1]
            br = jnp.concatenate([drecv[j, 0], drecv[j + 1, 0]], axis=1)
            bi = jnp.concatenate([drecv[j, 1], drecv[j + 1, 1]], axis=1)
            out_ref[0, :, columns] = (dot(ar, br) - dot(ai, bi)).astype(bf16)
            out_ref[1, :, columns] = (dot(ar, bi) + dot(ai, br)).astype(bf16)

        @when((site > 0) & ~odd)
        def _():
            loop(CHUNKS // 2, step_pair)

        @when((site > 0) & odd)
        def _():
            loop(CHUNKS, step)

        when(edge & ~odd)(drain_sent)


def shards(forward_props):
    x = forward_props[:, 0]
    _, rows, width = x.shape
    cols = width // CHUNKS
    dma = pltpu.SemaphoreType.DMA
    tm_size = lax.axis_size("tm")
    out = pl.pallas_call(
        functools.partial(kernel, tm_size),
        out_shape=jax.ShapeDtypeStruct(x.shape, bf16),
        in_specs=[pl.BlockSpec(memory_space=pl.ANY)],
        out_specs=pl.BlockSpec(memory_space=pltpu.VMEM),
        scratch_shapes=[
            pltpu.VMEM(x.shape, bf16),
            pltpu.VMEM((2, width, width), bf16),
            pltpu.VMEM((2, width, width), bf16),
            pltpu.VMEM((CHUNKS, 2, width, cols), bf16),
            pltpu.VMEM((CHUNKS, 2, width, cols), bf16),
            pltpu.VMEM((CHUNKS, 2, width, cols), bf16),
            pltpu.VMEM(x.shape, bf16),
            pltpu.VMEM(x.shape, bf16),
            pltpu.VMEM(x.shape, f32),
            dma((CHUNKS + 1,)),
            dma((PANELS, BANDS)),
            dma((PANELS, BANDS)),
            dma((PANELS, BANDS)),
            dma((PANELS, BANDS)),
            dma((PANELS, BANDS)),
            dma((PANELS, CHUNKS)),
            dma((PANELS, CHUNKS)),
            dma((PANELS, CHUNKS)),
            dma((CHUNKS,)),
            dma((CHUNKS,)),
            dma((CHUNKS,)),
            dma((CHUNKS,)),
            pltpu.VMEM(x.shape, bf16),
            dma((BANDS,)),
            dma((BANDS,)),
            dma((2, 2 * PANELS)),
            dma((2, 2 * PANELS)),
            pltpu.VMEM((2, width, 2 * cols), bf16),
        ],
        compiler_params=pltpu.CompilerParams(
            collective_id=0, has_side_effects=True, vmem_limit_bytes=52 * 2**20
        ),
        name="prefix_products",
    )(x)
    return out[:, None]


def solution(mesh):
    placed = (P(None, "tm", "panel", None),)
    return jax.shard_map(
        shards, mesh=mesh, in_specs=placed, out_specs=P(None, "tm", "panel", None), check_vma=False
    )
```

```python
import functools

import jax
import jax.numpy as jnp
from jax import lax
from jax.experimental import pallas as pl
from jax.experimental.pallas import tpu as pltpu
from jax.sharding import PartitionSpec as P

PANELS = 4
CHUNKS = 8
PIECES = 2 * PANELS
HELD = 4
EARLY = 4
BANDS = 4

bf16, f32 = jnp.bfloat16, jnp.float32


def dot(a, b):
    return jnp.dot(a, b, preferred_element_type=f32)


def when(cond):
    return pl.when(cond)


def loop(n, body):
    def step(i, carry):
        body(i)
        return carry

    lax.fori_loop(0, n, step, 0)


def kernel(
    tm_size, x_ref, out_ref, own, obuf, o2buf, ebuf, dsend, drecv, dloc, gbuf, acc,
    in_sem, o_recv, o_right, o_left, o_z, o2_recv, e_recv, e_right, e_left, e_in, d_recv, d_out, d_in,
    relay, relay_recv, relay_out, rows_recv, rows_out, wide,
):
    rows, width = x_ref.shape[1], x_ref.shape[2]
    cols = width // CHUNKS
    band = rows // BANDS
    tm, p = lax.axis_index("tm"), lax.axis_index("panel")
    core = lax.rem(tm, 2)
    site, sites = tm // 2, tm_size // 2

    def at(shift, panel):
        return (lax.rem(tm + shift + tm_size, tm_size), panel)

    def remote(src, dst, send, recv, where):
        return pltpu.make_async_remote_copy(
            src_ref=src, dst_ref=dst, send_sem=send, recv_sem=recv,
            device_id=where, device_id_type=pl.DeviceIdType.MESH,
        )

    def o_rows(q, c):
        return pl.ds(pl.multiple_of(q * rows + c * band, band), band)

    def o_copy(q, c, sems, where, dst=None, recv=None):
        piece = obuf.at[:, o_rows(q, c), :]
        target = piece if dst is None else dst.at[:, o_rows(q, c), :]
        arrive = (o_recv if recv is None else recv).at[q, c]
        return remote(piece, target, sems.at[q, c], arrive, where)

    def o_r(q, c):
        return o_copy(q, c, o_right, at(0, lax.rem(p + 1, PANELS)))

    def o_l(q, c):
        return o_copy(q, c, o_left, at(0, lax.rem(p + PANELS - 1, PANELS)))

    def o_up(q, c):
        return o_copy(q, c, o_z, at(3, p), o2buf, o2_recv)

    def o_aside(c):
        here = pl.ds(pl.multiple_of(c * band, band), band)
        return remote(
            obuf.at[:, o_rows(p, c), :], relay.at[:, here, :], o_z.at[p, c], relay_recv.at[c], at(5, PANELS - 1 - p)
        )

    def o_aside_on(c):
        here = pl.ds(pl.multiple_of(c * band, band), band)
        q = PANELS - 1 - p
        return remote(relay.at[:, here, :], o2buf.at[:, o_rows(q, c), :], relay_out.at[c], o2_recv.at[q, c], at(-2, q))

    def e_piece(q, j):
        return ebuf.at[j, :, pl.ds(pl.multiple_of(q * rows, rows), rows), :]

    def e_copy(q, j, sems, panel):
        return remote(e_piece(q, j), e_piece(q, j), sems.at[q, j], e_recv.at[q, j], at(0, panel))

    def e_r(q, j):
        return e_copy(q, j, e_right, lax.rem(p + 1, PANELS))

    def e_l(q, j):
        return e_copy(q, j, e_left, lax.rem(p + PANELS - 1, PANELS))

    def e_over(j):
        return remote(e_piece(p, j), e_piece(p, j), e_in.at[j], e_recv.at[p, j], at(1, p))

    def pair(q, j, sems, shift, panel):
        view = ebuf.at[pl.ds(j, 2), :, pl.ds(pl.multiple_of(q * rows, rows), rows), :]
        return remote(view, view, sems.at[q, j], e_recv.at[q, j], at(shift, panel))

    def pair_r(q, b, shift=0):
        return pair(q, 2 * b, e_right, shift, lax.rem(p + 1, PANELS))

    def pair_l(q, b, shift=0):
        return pair(q, CHUNKS - 2 - 2 * b, e_left, shift, lax.rem(p + PANELS - 1, PANELS))

    def d_next(j):
        return remote(dsend.at[j], drecv.at[j], d_out.at[j], d_recv.at[j], at(1, PANELS - 1 - p))

    def d_pass(j, panel):
        return remote(drecv.at[j], drecv.at[j], d_out.at[j], d_recv.at[j], at(0, panel))

    def d_over(j):
        return remote(drecv.at[j], drecv.at[j], d_in.at[j], d_recv.at[j], at(1, p))

    def piece(half, g, k, n):
        first = 2 * g
        q = jnp.where(half == 0, PANELS - 1 - k // 2, k // 2)
        j = jnp.where(half == 0, first, CHUNKS - first - n)
        part = rows // 2
        start = pl.multiple_of(q * rows + lax.rem(k, 2) * part, part)
        return pl.ds(j, n), slice(None), pl.ds(start, part), slice(None)

    def rows_next(half, g, k):
        view = piece(half, g, k, 2)
        m = PIECES * g + k
        return remote(
            dsend.at[view], drecv.at[view], rows_out.at[half, m], rows_recv.at[half, m], at(1, PANELS - 1 - p)
        )

    def rows_pass(half, g, k, n, panel):
        view = piece(half, g, k, n)
        m = PIECES * g + k
        return remote(drecv.at[view], drecv.at[view], rows_out.at[half, m], rows_recv.at[half, m], at(0, panel))

    odd = lax.rem(site, 2) == 1
    direct_out = jnp.where(odd, 6, 7)
    direct_in = jnp.where(odd, 7, 6)
    edge = (p == 0) | (p == PANELS - 1)
    low = p < PANELS // 2

    def pick(i, values):
        found = values[-1]
        for n in range(len(values) - 1):
            found = jnp.where(i == n, values[n], found)
        return found

    def arrival(i):
        inner = jnp.where(odd, pick(i, (0, 1, 7, 2, 6, 3, 5, 4)), pick(i, (0, 1, 2, 3, 7, 6, 5, 4)))
        outer = pick(i, (0, 1, 2, 3, 4, 7, 6, 5))
        a = jnp.where(edge, outer, inner)
        j = jnp.where(low, a, CHUNKS - 1 - a)
        return a, j

    def passes(a):
        return jnp.where(edge, a < 5, (a < 3) | (a >= direct_in))

    def pass_to(a):
        onward = jnp.where(edge, jnp.where(low, 1, 2), jnp.where(low, 2, 1))
        back = jnp.where(low, 0, PANELS - 1)
        return jnp.where(~edge & (a >= direct_in), back, onward)

    def load_chunk(j):
        columns = pl.ds(pl.multiple_of(j * cols, cols), cols)
        return pltpu.make_async_copy(x_ref.at[:, :, columns], e_piece(p, j), in_sem.at[j])

    load_e = pltpu.make_async_copy(x_ref, own, in_sem.at[CHUNKS])
    load_o = pltpu.make_async_copy(
        x_ref, obuf.at[:, pl.ds(pl.multiple_of(p * rows, rows), rows), :], in_sem.at[CHUNKS]
    )

    @when(core == 0)
    def _():
        loop(CHUNKS, lambda j: load_chunk(j).start())
        load_e.start()

    when(core == 1)(load_o.start)

    barrier = pltpu.get_barrier_semaphore()

    def greet(where):
        pl.semaphore_signal(barrier, inc=1, device_id=where, device_id_type=pl.DeviceIdType.MESH)

    @when(p > 0)
    def _():
        greet(at(0, p - 1))

    @when(p < PANELS - 1)
    def _():
        greet(at(0, p + 1))

    @when(core == 0)
    def _():
        greet(at(-3, p))

        @when(edge)
        def _():
            greet(at(-1, PANELS - 1 - p))

        @when(edge & odd)
        def _():
            greet(at(-5, PANELS - 1 - p))

        @when(edge & ~odd)
        def _():
            greet(at(2, PANELS - 1 - p))

    @when(core == 1)
    def _():
        greet(at(-1, p))

        @when(odd & (p > 0))
        def _():
            greet(at(-1, p - 1))

        @when(odd & (p < PANELS - 1))
        def _():
            greet(at(-1, p + 1))


    @when(core == 0)
    def _():
        loop(CHUNKS, lambda j: load_chunk(j).wait())

    when(core == 1)(load_o.wait)
    heard = jnp.where(edge & ~odd, jnp.where(core == 0, 2, 4), 3)
    pl.semaphore_wait(barrier, heard + jnp.where((core == 0) & odd, jnp.where(edge, 1, 2), 0))

    @when(core == 0)
    def _():
        @when(odd & (p < PANELS - 1))
        def _():
            loop(EARLY // 2, lambda b: pair_r(p, b, 1).start())

        @when(odd & (p > 0))
        def _():
            loop(EARLY // 2, lambda b: pair_l(p, b, 1).start())

        loop(CHUNKS, lambda j: e_over(j).start())
        load_e.wait()
        acc[...] = jnp.zeros_like(acc)

        @when(edge & odd & (site > 2))
        def _():
            def hand_on(c):
                o_aside(c).wait_recv()
                o_aside_on(c).start()

            loop(BANDS, hand_on)

        def take(i):
            come(i)
            multiply(i)

        def come(i):
            a, j = arrival(i)
            d_over(j).wait_recv()

            @when(passes(a) & ~held(a))
            def _():
                d_pass(j, pass_to(a)).start()

            d_over(j).start()

        def held(a):
            return odd & ~edge & (a == 7)

        def multiply(i):
            _, j = arrival(i)
            columns = pl.ds(pl.multiple_of(j * cols, cols), cols)
            dr, di = drecv[j, 0], drecv[j, 1]
            both = dot(own[0], jnp.concatenate([dr, di], axis=1)) + dot(own[1], jnp.concatenate([-di, dr], axis=1))
            gbuf[0, :, columns] = both[:, :cols].astype(bf16)
            gbuf[1, :, columns] = both[:, cols:].astype(bf16)

        def add(i, final=False):
            _, j = arrival(i)

            def rows_in(n):
                o_copy(j // 2, 2 * lax.rem(j, 2) + n, o_z, at(-3, p), o2buf, o2_recv).wait_recv()

            loop(BANDS // 2, rows_in)
            columns = pl.ds(pl.multiple_of(j * cols, cols), cols)
            gr, gi = gbuf[0, :, columns], gbuf[1, :, columns]
            below = jnp.concatenate([o2buf[0, columns, :], o2buf[1, columns, :]], axis=0)
            re = acc[0] + dot(jnp.concatenate([gr, -gi], axis=1), below)
            im = acc[1] + dot(jnp.concatenate([gi, gr], axis=1), below)
            if final:
                out_ref[0] = re.astype(bf16)
                out_ref[1] = im.astype(bf16)
            else:
                acc[0] = re
                acc[1] = im

        def pair_of(g):
            return jnp.where(low, 2 * g, CHUNKS - 2 - 2 * g)

        def multiply_pair(g):
            j = pair_of(g)
            columns = pl.ds(pl.multiple_of(j * cols, cols), 2 * cols)
            er, ei = own[0], own[1]
            dr = jnp.concatenate([drecv[j, 0], drecv[j + 1, 0]], axis=1)
            di = jnp.concatenate([drecv[j, 1], drecv[j + 1, 1]], axis=1)
            gbuf[0, :, columns] = (dot(er, dr) - dot(ei, di)).astype(bf16)
            gbuf[1, :, columns] = (dot(er, di) + dot(ei, dr)).astype(bf16)

        def add_pair(g, final=False):
            j = pair_of(g)
            loop(BANDS, lambda c: o_copy(j // 2, c, o_z, at(-3, p), o2buf, o2_recv).wait_recv())
            columns = pl.ds(pl.multiple_of(j * cols, cols), 2 * cols)
            gr, gi = gbuf[0, :, columns], gbuf[1, :, columns]
            tr, ti = o2buf[0, columns, :], o2buf[1, columns, :]
            re = acc[0] + (dot(gr, tr) - dot(gi, ti))
            im = acc[1] + (dot(gr, ti) + dot(gi, tr))
            if final:
                out_ref[0] = re.astype(bf16)
                out_ref[1] = im.astype(bf16)
            else:
                acc[0] = re
                acc[1] = im

        def added(i):
            return jnp.where(i < 3, 0, jnp.where(i < 6, 2 * i - 5, i))

        def step(i):
            take(i)

            @when(odd & ~edge & (i == 5))
            def _():
                d_pass(jnp.where(low, 7, 0), pass_to(7)).start()

            def more(n, carry):
                add(n)
                return carry

            @when(site > 1)
            def _():
                lax.fori_loop(added(i - 1), added(i), more, 0)

        def drain(i):
            a, j = arrival(i)
            d_over(j).wait_send()

            @when(passes(a))
            def _():
                d_pass(j, 1).wait_send()

        main = jnp.where(low, 0, 1)
        other = 1 - main

        def span(first, end, f):
            loop(end - first, lambda i: f(first + i))

        def give_back(k):
            def one(n, carry):
                rows_pass(other, 0, n, 2, pass_to(7)).start()
                return carry

            lax.fori_loop(jnp.where(k == HELD, 0, k), jnp.where(k < HELD, k, k + 1), one, 0)

        def take_rows(k):
            @when(edge)
            def _():
                for g in range(2):
                    rows_pass(main, g, k, 2, pass_to(0)).wait_recv()
                    rows_pass(main, g, k, 2, pass_to(0)).start()

            @when(~edge)
            def _():
                for g in range(2):
                    rows_pass(main, g, k, 2, pass_to(0)).wait_recv()
                    rows_pass(main, g, k, 2 - g, pass_to(0)).start()
                for g in range(2):
                    rows_pass(other, g, k, 2 - g, pass_to(0)).wait_recv()
                    if g == 0:
                        give_back(k)

        def drain_rows(k):
            rows_pass(main, 0, k, 2, pass_to(0)).wait_send()

            @when(edge)
            def _():
                rows_pass(main, 1, k, 2, pass_to(0)).wait_send()

            @when(~edge)
            def _():
                rows_pass(main, 1, k, 1, pass_to(0)).wait_send()
                rows_pass(other, 0, k, 2, pass_to(7)).wait_send()

        def over(i):
            d_over(arrival(i)[1]).start()

        loop(CHUNKS, lambda j: e_over(j).wait_send())

        @when(odd & (p < PANELS - 1))
        def _():
            loop(EARLY // 2, lambda b: pair_r(p, b, 1).wait_send())

        @when(odd & (p > 0))
        def _():
            loop(EARLY // 2, lambda b: pair_l(p, b, 1).wait_send())

        @when(edge & odd & (site > 2))
        def _():
            loop(BANDS, lambda c: o_aside_on(c).wait_send())

        @when(site == 0)
        def _():
            out_ref[...] = own[...]

        @when((site > 0) & odd)
        def _():
            loop(CHUNKS, step)
            loop(CHUNKS, drain)

        @when((site > 0) & ~odd)
        def _():
            loop(PIECES, take_rows)
            span(0, 4, over)

            @when(~edge)
            def _():
                span(4, 7, over)

            loop(2, multiply_pair)

            @when(edge)
            def _():
                come(4)
                loop(2, add_pair)
                loop(PIECES, lambda k: rows_pass(other, 0, k, 2, pass_to(0)).wait_recv())
                span(5, 7, over)
                come(7)

            multiply_pair(3)

            @when(~edge)
            def _():
                loop(2, add_pair)

            add_pair(3)

            @when(~edge)
            def _():
                come(7)

            loop(PIECES, drain_rows)
            multiply_pair(2)
            add_pair(2, final=True)

        @when(site == 1)
        def _():
            out_ref[...] = gbuf[...]

        @when((site > 1) & odd)
        def _():
            add(CHUNKS - 1, final=True)

        @when((site > 0) & ~odd)
        def _():
            loop(CHUNKS, lambda j: d_over(j).wait_send())

            @when(edge)
            def _():
                d_pass(arrival(4)[1], 1).wait_send()

    @when(core == 1)
    def _():
        def pass_o(q, c, right, left):
            @when(right & (p < PANELS - 1))
            def _():
                o_r(q, c).start()

            @when(left & (p > 0))
            def _():
                o_l(q, c).start()

            aside = edge & ~odd & (q == p)

            @when((site < sites - 2) & ~aside)
            def _():
                o_up(q, c).start()

            @when((site < sites - 2) & aside)
            def _():
                o_aside(c).start()

        def hop_band(n, c):
            @when(p - 1 - n >= 0)
            def _():
                o_r(p - 1 - n, c).wait_recv()
                pass_o(p - 1 - n, c, True, False)

            @when(p + 1 + n < PANELS)
            def _():
                o_l(p + 1 + n, c).wait_recv()
                pass_o(p + 1 + n, c, False, True)

        def hop(n):
            loop(BANDS, lambda c: hop_band(n, c))

        def own_e():
            loop(CHUNKS, lambda j: e_over(j).wait_recv())

        def nth(i):
            return jnp.where(p == 0, CHUNKS - 1 - i, i)

        def product(q, j):
            here = pl.ds(pl.multiple_of(q * rows, rows), rows)
            ar, ai = obuf[0, here, :], obuf[1, here, :]
            br, bi = ebuf[j, 0], ebuf[j, 1]
            re = (dot(ar, br) - dot(ai, bi)).astype(bf16)
            im = (dot(ar, bi) + dot(ai, br)).astype(bf16)
            return re, im

        def two(j, part):
            return jnp.concatenate([ebuf[j, part], ebuf[j + 1, part]], axis=1)

        def rows_of(q, b, j):
            here = pl.ds(pl.multiple_of(q * rows + b * (rows // 2), rows // 2), rows // 2)
            ar, ai = obuf[0, here, :], obuf[1, here, :]
            br, bi = two(j, 0), two(j, 1)
            re = (dot(ar, br) - dot(ai, bi)).astype(bf16)
            im = (dot(ar, bi) + dot(ai, br)).astype(bf16)
            for n in range(2):
                dsend[j + n, 0, here, :] = re[:, n * cols : (n + 1) * cols]
                dsend[j + n, 1, here, :] = im[:, n * cols : (n + 1) * cols]

        def e_in_chunk(j):
            @when(p == 0)
            def _():
                loop(PANELS - 1, lambda q: e_l(q + 1, j).wait_recv())

            @when(p == 3)
            def _():
                loop(PANELS - 1, lambda q: e_r(q, j).wait_recv())

        def copy_own(j):
            mine = pl.ds(pl.multiple_of(p * rows, rows), rows)
            dloc[:, :, pl.ds(pl.multiple_of(j * cols, cols), cols)] = dsend[j, :, mine, :]

        def own_chunk(j):
            columns = pl.ds(pl.multiple_of(j * cols, cols), cols)
            re, im = product(p, j)
            dloc[0, :, columns] = re
            dloc[1, :, columns] = im

        def whole_chunk(i):
            j = nth(i)
            e_in_chunk(j)

            def block(q):
                here = pl.ds(pl.multiple_of(q * rows, rows), rows)
                both = (dot(obuf[0, here, :], wide[0]) + dot(obuf[1, here, :], wide[1])).astype(bf16)
                dsend[j, 0, here, :] = both[:, :cols]
                dsend[j, 1, here, :] = both[:, cols:]

            @when(i < direct_out)
            def _():
                wide[0] = jnp.concatenate([ebuf[j, 0], ebuf[j, 1]], axis=1)
                wide[1] = jnp.concatenate([-ebuf[j, 1], ebuf[j, 0]], axis=1)
                loop(PANELS, block)

                @when(site < sites - 1)
                def _():
                    d_next(j).start()

                copy_own(j)

            @when(i >= direct_out)
            def _():
                own_chunk(j)

        @when(~odd)
        def _():
            loop(BANDS, lambda c: pass_o(p, c, True, True))
            hop(0)
            own_e()

            @when(p == 0)
            def _():
                loop(CHUNKS, lambda j: e_r(0, j).start())

            @when(p == 3)
            def _():
                loop(CHUNKS, lambda j: e_l(3, CHUNKS - 1 - j).start())

            hop(1)

            @when(p == 1)
            def _():
                def one(j):
                    e_r(1, j).start()
                    e_r(0, j).wait_recv()
                    e_r(0, j).start()

                loop(CHUNKS, one)

            @when(p == 2)
            def _():
                def one(i):
                    j = CHUNKS - 1 - i
                    e_l(2, j).start()
                    e_l(3, j).wait_recv()
                    e_l(3, j).start()

                loop(CHUNKS, one)

            hop(2)

            @when(p == 1)
            def _():
                def one(i):
                    j = CHUNKS - 1 - i
                    e_l(1, j).start()
                    e_l(2, j).wait_recv()
                    e_l(2, j).start()
                    e_l(3, j).wait_recv()
                    e_l(3, j).start()

                loop(CHUNKS, one)

            @when(p == 2)
            def _():
                def one(j):
                    e_r(2, j).start()
                    e_r(1, j).wait_recv()
                    e_r(1, j).start()
                    e_r(0, j).wait_recv()
                    e_r(0, j).start()

                loop(CHUNKS, one)

            @when(edge)
            def _():
                loop(CHUNKS, whole_chunk)

        sent = jnp.where(p == 0, 1, 0)

        @when(odd)
        def _():
            def pass_e(q, b, right, left):
                @when(right & (p < PANELS - 1))
                def _():
                    pair_r(q, b).start()

                @when(left & (p > 0))
                def _():
                    pair_l(q, b).start()

            def own_o(n):
                def one(c):
                    @when((p == n) & (p < PANELS - 1))
                    def _():
                        o_r(p, c).start()

                    @when((p == PANELS - 1 - n) & (p > 0))
                    def _():
                        o_l(p, c).start()

                loop(BANDS, one)

            @when(site < sites - 2)
            def _():
                loop(BANDS, lambda c: o_up(p, c).start())

            for n in range(PANELS - 1):
                def one(b):
                    @when(p - 1 - n >= 0)
                    def _():
                        pair_r(p - 1 - n, b).wait_recv()
                        pass_e(p - 1 - n, b, True, False)

                    @when(p + 1 + n < PANELS)
                    def _():
                        pair_l(p + 1 + n, b).wait_recv()
                        pass_e(p + 1 + n, b, False, True)

                loop(EARLY // 2, one)
                if n == 0:
                    own_o(0)
                own_o(n + 1)

            def send_rows(k):
                @when(edge)
                def _():
                    def one(g):
                        q = jnp.where(p == 0, k // 2, PANELS - 1 - k // 2)
                        rows_of(q, lax.rem(k, 2), jnp.where(p == 0, CHUNKS - 2 - 2 * g, 2 * g))

                        @when(site < sites - 1)
                        def _():
                            for n in range(2):
                                when(g == n)(rows_next(sent, n, k).start)

                    loop(2, one)

            def hop_and_send(n):
                def half(b):
                    loop(BANDS // 2, lambda c: hop_band(n, b * (BANDS // 2) + c))
                    send_rows(2 * n + 2 + b)

                loop(2, half)

            own_e()
            loop(2, send_rows)
            hop_and_send(0)

            @when(p == 0)
            def _():
                loop(EARLY, lambda i: e_r(0, EARLY + i).start())

            @when(p == 3)
            def _():
                loop(EARLY, lambda i: e_l(3, EARLY - 1 - i).start())

            hop_and_send(1)

            @when(p == 1)
            def _():
                def one(i):
                    j = EARLY + i
                    e_r(1, j).start()
                    e_r(0, j).wait_recv()
                    e_r(0, j).start()

                loop(EARLY, one)

            @when(p == 2)
            def _():
                def one(i):
                    j = EARLY - 1 - i
                    e_l(2, j).start()
                    e_l(3, j).wait_recv()
                    e_l(3, j).start()

                loop(EARLY, one)

            hop_and_send(2)

            @when(p == 1)
            def _():
                def one(i):
                    j = EARLY - 1 - i
                    e_l(1, j).start()
                    e_l(2, j).wait_recv()
                    e_l(2, j).start()
                    e_l(3, j).wait_recv()
                    e_l(3, j).start()

                loop(EARLY, one)

            @when(p == 2)
            def _():
                def one(i):
                    j = EARLY + i
                    e_r(2, j).start()
                    e_r(1, j).wait_recv()
                    e_r(1, j).start()
                    e_r(0, j).wait_recv()
                    e_r(0, j).start()

                loop(EARLY, one)

            @when(edge)
            def _():
                loop(EARLY, lambda i: whole_chunk(EARLY + i))
                loop(EARLY, lambda i: copy_own(nth(i)))

        @when(~edge)
        def _():
            loop(CHUNKS, own_chunk)

        def drain_o(i):
            q, c = i // BANDS, lax.rem(i, BANDS)

            @when(site < sites - 2)
            def _():
                o_up(q, c).wait_send()

            @when((q <= p) & (p < PANELS - 1))
            def _():
                o_r(q, c).wait_send()

            @when((q >= p) & (p > 0))
            def _():
                o_l(q, c).wait_send()

        loop(PANELS * BANDS, drain_o)

        def drain_e(i):
            q, j = i // CHUNKS, lax.rem(i, CHUNKS)

            @when((q <= p) & (p < PANELS - 1))
            def _():
                @when(~odd | (j >= EARLY))
                def _():
                    e_r(q, j).wait_send()

                @when(odd & (q < p) & (j < EARLY // 2))
                def _():
                    pair_r(q, j).wait_send()

            @when((q >= p) & (p > 0))
            def _():
                @when(~odd | (j < EARLY))
                def _():
                    e_l(q, j).wait_send()

                @when(odd & (q > p) & (j >= EARLY) & (j < EARLY + EARLY // 2))
                def _():
                    pair_l(q, j - EARLY).wait_send()

        loop(PANELS * CHUNKS, drain_e)

        def step(i):
            _, j = arrival(i)
            d_over(j).wait_recv()
            columns = pl.ds(pl.multiple_of(j * cols, cols), cols)
            br, bi = drecv[j, 0], drecv[j, 1]
            both = dot(dloc[0], jnp.concatenate([br, bi], axis=1)) + dot(dloc[1], jnp.concatenate([-bi, br], axis=1))
            re, im = both[:, :cols].astype(bf16), both[:, cols:].astype(bf16)
            out_ref[0, :, columns] = re
            out_ref[1, :, columns] = im

        def drain_sent():
            def drain_d(i):
                @when((i < direct_out) & (site < sites - 1) & (~odd | (i >= EARLY)))
                def _():
                    d_next(nth(i)).wait_send()

            loop(CHUNKS, drain_d)

            @when(odd & (site < sites - 1))
            def _():
                for g in range(2):
                    loop(PIECES, lambda k: rows_next(sent, g, k).wait_send())

        when(edge & odd)(drain_sent)

        @when(site == 0)
        def _():
            out_ref[...] = dloc[...]

        def step_pair(i):
            g = pick(i, (0, 1, 3, 2))
            j = jnp.where(low, 2 * g, CHUNKS - 2 - 2 * g)
            loop(2, lambda n: d_over(j + n).wait_recv())
            columns = pl.ds(pl.multiple_of(j * cols, cols), 2 * cols)
            ar, ai = dloc[0], dloc[1]
            br = jnp.concatenate([drecv[j, 0], drecv[j + 1, 0]], axis=1)
            bi = jnp.concatenate([drecv[j, 1], drecv[j + 1, 1]], axis=1)
            out_ref[0, :, columns] = (dot(ar, br) - dot(ai, bi)).astype(bf16)
            out_ref[1, :, columns] = (dot(ar, bi) + dot(ai, br)).astype(bf16)

        @when((site > 0) & ~odd)
        def _():
            loop(CHUNKS // 2, step_pair)

        @when((site > 0) & odd)
        def _():
            loop(CHUNKS, step)

        when(edge & ~odd)(drain_sent)


def shards(forward_props):
    x = forward_props[:, 0]
    _, rows, width = x.shape
    cols = width // CHUNKS
    dma = pltpu.SemaphoreType.DMA
    tm_size = lax.axis_size("tm")
    out = pl.pallas_call(
        functools.partial(kernel, tm_size),
        out_shape=jax.ShapeDtypeStruct(x.shape, bf16),
        in_specs=[pl.BlockSpec(memory_space=pl.ANY)],
        out_specs=pl.BlockSpec(memory_space=pltpu.VMEM),
        scratch_shapes=[
            pltpu.VMEM(x.shape, bf16),
            pltpu.VMEM((2, width, width), bf16),
            pltpu.VMEM((2, width, width), bf16),
            pltpu.VMEM((CHUNKS, 2, width, cols), bf16),
            pltpu.VMEM((CHUNKS, 2, width, cols), bf16),
            pltpu.VMEM((CHUNKS, 2, width, cols), bf16),
            pltpu.VMEM(x.shape, bf16),
            pltpu.VMEM(x.shape, bf16),
            pltpu.VMEM(x.shape, f32),
            dma((CHUNKS + 1,)),
            dma((PANELS, BANDS)),
            dma((PANELS, BANDS)),
            dma((PANELS, BANDS)),
            dma((PANELS, BANDS)),
            dma((PANELS, BANDS)),
            dma((PANELS, CHUNKS)),
            dma((PANELS, CHUNKS)),
            dma((PANELS, CHUNKS)),
            dma((CHUNKS,)),
            dma((CHUNKS,)),
            dma((CHUNKS,)),
            dma((CHUNKS,)),
            pltpu.VMEM(x.shape, bf16),
            dma((BANDS,)),
            dma((BANDS,)),
            dma((2, 2 * PIECES)),
            dma((2, 2 * PIECES)),
            pltpu.VMEM((2, width, 2 * cols), bf16),
        ],
        compiler_params=pltpu.CompilerParams(
            collective_id=0, has_side_effects=True, vmem_limit_bytes=52 * 2**20
        ),
        name="prefix_products",
    )(x)
    return out[:, None]


def solution(mesh):
    placed = (P(None, "tm", "panel", None),)
    return jax.shard_map(
        shards, mesh=mesh, in_specs=placed, out_specs=P(None, "tm", "panel", None), check_vma=False
    )
```

```python
import functools

import jax
import jax.numpy as jnp
from jax import lax
from jax.experimental import pallas as pl
from jax.experimental.pallas import tpu as pltpu
from jax.sharding import PartitionSpec as P

PANELS = 4
CHUNKS = 8
PIECES = 2 * PANELS
GIVEN = (0, 0, 0, 0, 1, 3, 6, 8)
EARLY = 4
BANDS = 4

bf16, f32 = jnp.bfloat16, jnp.float32


def dot(a, b):
    return jnp.dot(a, b, preferred_element_type=f32)


def when(cond):
    return pl.when(cond)


def loop(n, body):
    def step(i, carry):
        body(i)
        return carry

    lax.fori_loop(0, n, step, 0)


def kernel(
    tm_size, x_ref, out_ref, own, obuf, o2buf, ebuf, dsend, drecv, dloc, gbuf, acc,
    in_sem, o_recv, o_right, o_left, o_z, o2_recv, e_recv, e_right, e_left, e_in, d_recv, d_out, d_in,
    relay, relay_recv, relay_out, rows_recv, rows_out, wide,
):
    rows, width = x_ref.shape[1], x_ref.shape[2]
    cols = width // CHUNKS
    band = rows // BANDS
    tm, p = lax.axis_index("tm"), lax.axis_index("panel")
    core = lax.rem(tm, 2)
    site, sites = tm // 2, tm_size // 2

    def at(shift, panel):
        return (lax.rem(tm + shift + tm_size, tm_size), panel)

    def remote(src, dst, send, recv, where):
        return pltpu.make_async_remote_copy(
            src_ref=src, dst_ref=dst, send_sem=send, recv_sem=recv,
            device_id=where, device_id_type=pl.DeviceIdType.MESH,
        )

    def o_rows(q, c):
        return pl.ds(pl.multiple_of(q * rows + c * band, band), band)

    def o_copy(q, c, sems, where, dst=None, recv=None):
        piece = obuf.at[:, o_rows(q, c), :]
        target = piece if dst is None else dst.at[:, o_rows(q, c), :]
        arrive = (o_recv if recv is None else recv).at[q, c]
        return remote(piece, target, sems.at[q, c], arrive, where)

    def o_r(q, c):
        return o_copy(q, c, o_right, at(0, lax.rem(p + 1, PANELS)))

    def o_l(q, c):
        return o_copy(q, c, o_left, at(0, lax.rem(p + PANELS - 1, PANELS)))

    def o_up(q, c):
        return o_copy(q, c, o_z, at(3, p), o2buf, o2_recv)

    def o_aside(c):
        here = pl.ds(pl.multiple_of(c * band, band), band)
        return remote(
            obuf.at[:, o_rows(p, c), :], relay.at[:, here, :], o_z.at[p, c], relay_recv.at[c], at(5, PANELS - 1 - p)
        )

    def o_aside_on(c):
        here = pl.ds(pl.multiple_of(c * band, band), band)
        q = PANELS - 1 - p
        return remote(relay.at[:, here, :], o2buf.at[:, o_rows(q, c), :], relay_out.at[c], o2_recv.at[q, c], at(-2, q))

    def e_piece(q, j):
        return ebuf.at[j, :, pl.ds(pl.multiple_of(q * rows, rows), rows), :]

    def e_copy(q, j, sems, panel):
        return remote(e_piece(q, j), e_piece(q, j), sems.at[q, j], e_recv.at[q, j], at(0, panel))

    def e_r(q, j):
        return e_copy(q, j, e_right, lax.rem(p + 1, PANELS))

    def e_l(q, j):
        return e_copy(q, j, e_left, lax.rem(p + PANELS - 1, PANELS))

    def e_over(j):
        return remote(e_piece(p, j), e_piece(p, j), e_in.at[j], e_recv.at[p, j], at(1, p))

    def pair(q, j, sems, shift, panel):
        view = ebuf.at[pl.ds(j, 2), :, pl.ds(pl.multiple_of(q * rows, rows), rows), :]
        return remote(view, view, sems.at[q, j], e_recv.at[q, j], at(shift, panel))

    def pair_r(q, b, shift=0):
        return pair(q, 2 * b, e_right, shift, lax.rem(p + 1, PANELS))

    def pair_l(q, b, shift=0):
        return pair(q, CHUNKS - 2 - 2 * b, e_left, shift, lax.rem(p + PANELS - 1, PANELS))

    def d_next(j):
        return remote(dsend.at[j], drecv.at[j], d_out.at[j], d_recv.at[j], at(1, PANELS - 1 - p))

    def d_pass(j, panel):
        return remote(drecv.at[j], drecv.at[j], d_out.at[j], d_recv.at[j], at(0, panel))

    def d_over(j):
        return remote(drecv.at[j], drecv.at[j], d_in.at[j], d_recv.at[j], at(1, p))

    def piece(half, g, k, n):
        first = 2 * g
        q = jnp.where(half == 0, PANELS - 1 - k // 2, k // 2)
        j = jnp.where(half == 0, first, CHUNKS - first - n)
        part = rows // 2
        start = pl.multiple_of(q * rows + lax.rem(k, 2) * part, part)
        return pl.ds(j, n), slice(None), pl.ds(start, part), slice(None)

    def rows_next(half, g, k):
        view = piece(half, g, k, 2)
        m = PIECES * g + k
        return remote(
            dsend.at[view], drecv.at[view], rows_out.at[half, m], rows_recv.at[half, m], at(1, PANELS - 1 - p)
        )

    def rows_pass(half, g, k, n, panel):
        view = piece(half, g, k, n)
        m = PIECES * g + k
        return remote(drecv.at[view], drecv.at[view], rows_out.at[half, m], rows_recv.at[half, m], at(0, panel))

    odd = lax.rem(site, 2) == 1
    direct_out = jnp.where(odd, 6, 7)
    direct_in = jnp.where(odd, 7, 6)
    edge = (p == 0) | (p == PANELS - 1)
    low = p < PANELS // 2

    def pick(i, values):
        found = values[-1]
        for n in range(len(values) - 1):
            found = jnp.where(i == n, values[n], found)
        return found

    def arrival(i):
        inner = jnp.where(odd, pick(i, (0, 1, 7, 2, 6, 3, 5, 4)), pick(i, (0, 1, 2, 3, 7, 6, 5, 4)))
        outer = pick(i, (0, 1, 2, 3, 4, 7, 6, 5))
        a = jnp.where(edge, outer, inner)
        j = jnp.where(low, a, CHUNKS - 1 - a)
        return a, j

    def passes(a):
        return jnp.where(edge, a < 5, (a < 3) | (a >= direct_in))

    def pass_to(a):
        onward = jnp.where(edge, jnp.where(low, 1, 2), jnp.where(low, 2, 1))
        back = jnp.where(low, 0, PANELS - 1)
        return jnp.where(~edge & (a >= direct_in), back, onward)

    def load_chunk(j):
        columns = pl.ds(pl.multiple_of(j * cols, cols), cols)
        return pltpu.make_async_copy(x_ref.at[:, :, columns], e_piece(p, j), in_sem.at[j])

    load_e = pltpu.make_async_copy(x_ref, own, in_sem.at[CHUNKS])
    load_o = pltpu.make_async_copy(
        x_ref, obuf.at[:, pl.ds(pl.multiple_of(p * rows, rows), rows), :], in_sem.at[CHUNKS]
    )

    @when(core == 0)
    def _():
        loop(CHUNKS, lambda j: load_chunk(j).start())
        load_e.start()

    when(core == 1)(load_o.start)

    barrier = pltpu.get_barrier_semaphore()

    def greet(where):
        pl.semaphore_signal(barrier, inc=1, device_id=where, device_id_type=pl.DeviceIdType.MESH)

    @when(p > 0)
    def _():
        greet(at(0, p - 1))

    @when(p < PANELS - 1)
    def _():
        greet(at(0, p + 1))

    @when(core == 0)
    def _():
        greet(at(-3, p))

        @when(edge)
        def _():
            greet(at(-1, PANELS - 1 - p))

        @when(edge & odd)
        def _():
            greet(at(-5, PANELS - 1 - p))

        @when(edge & ~odd)
        def _():
            greet(at(2, PANELS - 1 - p))

    @when(core == 1)
    def _():
        greet(at(-1, p))

        @when(odd & (p > 0))
        def _():
            greet(at(-1, p - 1))

        @when(odd & (p < PANELS - 1))
        def _():
            greet(at(-1, p + 1))


    @when(core == 0)
    def _():
        loop(CHUNKS, lambda j: load_chunk(j).wait())

    when(core == 1)(load_o.wait)
    heard = jnp.where(edge & ~odd, jnp.where(core == 0, 2, 4), 3)
    pl.semaphore_wait(barrier, heard + jnp.where((core == 0) & odd, jnp.where(edge, 1, 2), 0))

    @when(core == 0)
    def _():
        @when(odd & (p < PANELS - 1))
        def _():
            loop(EARLY // 2, lambda b: pair_r(p, b, 1).start())

        @when(odd & (p > 0))
        def _():
            loop(EARLY // 2, lambda b: pair_l(p, b, 1).start())

        loop(CHUNKS, lambda j: e_over(j).start())
        load_e.wait()
        acc[...] = jnp.zeros_like(acc)

        @when(edge & odd & (site > 2))
        def _():
            def hand_on(c):
                o_aside(c).wait_recv()
                o_aside_on(c).start()

            loop(BANDS, hand_on)

        def take(i):
            come(i)
            multiply(i)

        def come(i):
            a, j = arrival(i)
            d_over(j).wait_recv()

            @when(passes(a) & ~held(a))
            def _():
                d_pass(j, pass_to(a)).start()

            d_over(j).start()

        def held(a):
            return odd & ~edge & (a == 7)

        def multiply(i):
            _, j = arrival(i)
            columns = pl.ds(pl.multiple_of(j * cols, cols), cols)
            dr, di = drecv[j, 0], drecv[j, 1]
            both = dot(own[0], jnp.concatenate([dr, di], axis=1)) + dot(own[1], jnp.concatenate([-di, dr], axis=1))
            gbuf[0, :, columns] = both[:, :cols].astype(bf16)
            gbuf[1, :, columns] = both[:, cols:].astype(bf16)

        def add(i, final=False):
            _, j = arrival(i)

            def rows_in(n):
                o_copy(j // 2, 2 * lax.rem(j, 2) + n, o_z, at(-3, p), o2buf, o2_recv).wait_recv()

            loop(BANDS // 2, rows_in)
            columns = pl.ds(pl.multiple_of(j * cols, cols), cols)
            gr, gi = gbuf[0, :, columns], gbuf[1, :, columns]
            below = jnp.concatenate([o2buf[0, columns, :], o2buf[1, columns, :]], axis=0)
            re = acc[0] + dot(jnp.concatenate([gr, -gi], axis=1), below)
            im = acc[1] + dot(jnp.concatenate([gi, gr], axis=1), below)
            if final:
                out_ref[0] = re.astype(bf16)
                out_ref[1] = im.astype(bf16)
            else:
                acc[0] = re
                acc[1] = im

        def pair_of(g):
            return jnp.where(low, 2 * g, CHUNKS - 2 - 2 * g)

        def multiply_pair(g):
            j = pair_of(g)
            columns = pl.ds(pl.multiple_of(j * cols, cols), 2 * cols)
            er, ei = own[0], own[1]
            dr = jnp.concatenate([drecv[j, 0], drecv[j + 1, 0]], axis=1)
            di = jnp.concatenate([drecv[j, 1], drecv[j + 1, 1]], axis=1)
            gbuf[0, :, columns] = (dot(er, dr) - dot(ei, di)).astype(bf16)
            gbuf[1, :, columns] = (dot(er, di) + dot(ei, dr)).astype(bf16)

        def add_pair(g, final=False):
            j = pair_of(g)
            loop(BANDS, lambda c: o_copy(j // 2, c, o_z, at(-3, p), o2buf, o2_recv).wait_recv())
            columns = pl.ds(pl.multiple_of(j * cols, cols), 2 * cols)
            gr, gi = gbuf[0, :, columns], gbuf[1, :, columns]
            tr, ti = o2buf[0, columns, :], o2buf[1, columns, :]
            re = acc[0] + (dot(gr, tr) - dot(gi, ti))
            im = acc[1] + (dot(gr, ti) + dot(gi, tr))
            if final:
                out_ref[0] = re.astype(bf16)
                out_ref[1] = im.astype(bf16)
            else:
                acc[0] = re
                acc[1] = im

        def added(i):
            return jnp.where(i < 3, 0, jnp.where(i < 6, 2 * i - 5, i))

        def step(i):
            take(i)

            @when(odd & ~edge & (i == 5))
            def _():
                d_pass(jnp.where(low, 7, 0), pass_to(7)).start()

            def more(n, carry):
                add(n)
                return carry

            @when(site > 1)
            def _():
                lax.fori_loop(added(i - 1), added(i), more, 0)

        def drain(i):
            a, j = arrival(i)
            d_over(j).wait_send()

            @when(passes(a))
            def _():
                d_pass(j, 1).wait_send()

        main = jnp.where(low, 0, 1)
        other = 1 - main

        def span(first, end, f):
            loop(end - first, lambda i: f(first + i))

        def give_back(k):
            def one(n, carry):
                rows_pass(other, 0, n, 2, pass_to(7)).start()
                return carry

            lax.fori_loop(pick(k, (0,) + GIVEN[:-1]), pick(k, GIVEN), one, 0)

        def take_rows(k):
            @when(edge)
            def _():
                for g in range(2):
                    rows_pass(main, g, k, 2, pass_to(0)).wait_recv()
                    rows_pass(main, g, k, 2, pass_to(0)).start()

            @when(~edge)
            def _():
                for g in range(2):
                    rows_pass(main, g, k, 2, pass_to(0)).wait_recv()
                    rows_pass(main, g, k, 2 - g, pass_to(0)).start()
                for g in range(2):
                    rows_pass(other, g, k, 2 - g, pass_to(0)).wait_recv()
                    if g == 0:
                        give_back(k)

        def drain_rows(k):
            rows_pass(main, 0, k, 2, pass_to(0)).wait_send()

            @when(edge)
            def _():
                rows_pass(main, 1, k, 2, pass_to(0)).wait_send()

            @when(~edge)
            def _():
                rows_pass(main, 1, k, 1, pass_to(0)).wait_send()
                rows_pass(other, 0, k, 2, pass_to(7)).wait_send()

        def over(i):
            d_over(arrival(i)[1]).start()

        loop(CHUNKS, lambda j: e_over(j).wait_send())

        @when(odd & (p < PANELS - 1))
        def _():
            loop(EARLY // 2, lambda b: pair_r(p, b, 1).wait_send())

        @when(odd & (p > 0))
        def _():
            loop(EARLY // 2, lambda b: pair_l(p, b, 1).wait_send())

        @when(edge & odd & (site > 2))
        def _():
            loop(BANDS, lambda c: o_aside_on(c).wait_send())

        @when(site == 0)
        def _():
            out_ref[...] = own[...]

        @when((site > 0) & odd)
        def _():
            loop(CHUNKS, step)
            loop(CHUNKS, drain)

        @when((site > 0) & ~odd)
        def _():
            loop(PIECES, take_rows)
            span(0, 4, over)

            @when(~edge)
            def _():
                span(4, 7, over)

            loop(2, multiply_pair)

            @when(edge)
            def _():
                come(4)
                loop(2, add_pair)
                loop(PIECES, lambda k: rows_pass(other, 0, k, 2, pass_to(0)).wait_recv())
                span(5, 7, over)
                come(7)

            multiply_pair(3)

            @when(~edge)
            def _():
                loop(2, add_pair)

            add_pair(3)

            @when(~edge)
            def _():
                come(7)

            loop(PIECES, drain_rows)
            multiply_pair(2)
            add_pair(2, final=True)

        @when(site == 1)
        def _():
            out_ref[...] = gbuf[...]

        @when((site > 1) & odd)
        def _():
            add(CHUNKS - 1, final=True)

        @when((site > 0) & ~odd)
        def _():
            loop(CHUNKS, lambda j: d_over(j).wait_send())

            @when(edge)
            def _():
                d_pass(arrival(4)[1], 1).wait_send()

    @when(core == 1)
    def _():
        def pass_o(q, c, right, left):
            @when(right & (p < PANELS - 1))
            def _():
                o_r(q, c).start()

            @when(left & (p > 0))
            def _():
                o_l(q, c).start()

            aside = edge & ~odd & (q == p)

            @when((site < sites - 2) & ~aside)
            def _():
                o_up(q, c).start()

            @when((site < sites - 2) & aside)
            def _():
                o_aside(c).start()

        def hop_band(n, c):
            @when(p - 1 - n >= 0)
            def _():
                o_r(p - 1 - n, c).wait_recv()
                pass_o(p - 1 - n, c, True, False)

            @when(p + 1 + n < PANELS)
            def _():
                o_l(p + 1 + n, c).wait_recv()
                pass_o(p + 1 + n, c, False, True)

        def hop(n):
            loop(BANDS, lambda c: hop_band(n, c))

        def own_e():
            loop(CHUNKS, lambda j: e_over(j).wait_recv())

        def nth(i):
            return jnp.where(p == 0, CHUNKS - 1 - i, i)

        def product(q, j):
            here = pl.ds(pl.multiple_of(q * rows, rows), rows)
            ar, ai = obuf[0, here, :], obuf[1, here, :]
            br, bi = ebuf[j, 0], ebuf[j, 1]
            re = (dot(ar, br) - dot(ai, bi)).astype(bf16)
            im = (dot(ar, bi) + dot(ai, br)).astype(bf16)
            return re, im

        def two(j, part):
            return jnp.concatenate([ebuf[j, part], ebuf[j + 1, part]], axis=1)

        def rows_of(q, b, j):
            here = pl.ds(pl.multiple_of(q * rows + b * (rows // 2), rows // 2), rows // 2)
            ar, ai = obuf[0, here, :], obuf[1, here, :]
            br, bi = two(j, 0), two(j, 1)
            re = (dot(ar, br) - dot(ai, bi)).astype(bf16)
            im = (dot(ar, bi) + dot(ai, br)).astype(bf16)
            for n in range(2):
                dsend[j + n, 0, here, :] = re[:, n * cols : (n + 1) * cols]
                dsend[j + n, 1, here, :] = im[:, n * cols : (n + 1) * cols]

        def e_in_chunk(j):
            @when(p == 0)
            def _():
                loop(PANELS - 1, lambda q: e_l(q + 1, j).wait_recv())

            @when(p == 3)
            def _():
                loop(PANELS - 1, lambda q: e_r(q, j).wait_recv())

        def copy_own(j):
            mine = pl.ds(pl.multiple_of(p * rows, rows), rows)
            dloc[:, :, pl.ds(pl.multiple_of(j * cols, cols), cols)] = dsend[j, :, mine, :]

        def own_chunk(j):
            columns = pl.ds(pl.multiple_of(j * cols, cols), cols)
            re, im = product(p, j)
            dloc[0, :, columns] = re
            dloc[1, :, columns] = im

        def whole_chunk(i):
            j = nth(i)
            e_in_chunk(j)

            def block(q):
                here = pl.ds(pl.multiple_of(q * rows, rows), rows)
                both = (dot(obuf[0, here, :], wide[0]) + dot(obuf[1, here, :], wide[1])).astype(bf16)
                dsend[j, 0, here, :] = both[:, :cols]
                dsend[j, 1, here, :] = both[:, cols:]

            @when(i < direct_out)
            def _():
                wide[0] = jnp.concatenate([ebuf[j, 0], ebuf[j, 1]], axis=1)
                wide[1] = jnp.concatenate([-ebuf[j, 1], ebuf[j, 0]], axis=1)
                loop(PANELS, block)

                @when(site < sites - 1)
                def _():
                    d_next(j).start()

                copy_own(j)

            @when(i >= direct_out)
            def _():
                own_chunk(j)

        @when(~odd)
        def _():
            loop(BANDS, lambda c: pass_o(p, c, True, True))
            hop(0)
            own_e()

            @when(p == 0)
            def _():
                loop(CHUNKS, lambda j: e_r(0, j).start())

            @when(p == 3)
            def _():
                loop(CHUNKS, lambda j: e_l(3, CHUNKS - 1 - j).start())

            hop(1)

            @when(p == 1)
            def _():
                def one(j):
                    e_r(1, j).start()
                    e_r(0, j).wait_recv()
                    e_r(0, j).start()

                loop(CHUNKS, one)

            @when(p == 2)
            def _():
                def one(i):
                    j = CHUNKS - 1 - i
                    e_l(2, j).start()
                    e_l(3, j).wait_recv()
                    e_l(3, j).start()

                loop(CHUNKS, one)

            hop(2)

            @when(p == 1)
            def _():
                def one(i):
                    j = CHUNKS - 1 - i
                    e_l(1, j).start()
                    e_l(2, j).wait_recv()
                    e_l(2, j).start()
                    e_l(3, j).wait_recv()
                    e_l(3, j).start()

                loop(CHUNKS, one)

            @when(p == 2)
            def _():
                def one(j):
                    e_r(2, j).start()
                    e_r(1, j).wait_recv()
                    e_r(1, j).start()
                    e_r(0, j).wait_recv()
                    e_r(0, j).start()

                loop(CHUNKS, one)

            @when(edge)
            def _():
                loop(CHUNKS, whole_chunk)

        sent = jnp.where(p == 0, 1, 0)

        @when(odd)
        def _():
            def pass_e(q, b, right, left):
                @when(right & (p < PANELS - 1))
                def _():
                    pair_r(q, b).start()

                @when(left & (p > 0))
                def _():
                    pair_l(q, b).start()

            def own_o(n):
                def one(c):
                    @when((p == n) & (p < PANELS - 1))
                    def _():
                        o_r(p, c).start()

                    @when((p == PANELS - 1 - n) & (p > 0))
                    def _():
                        o_l(p, c).start()

                loop(BANDS, one)

            @when(site < sites - 2)
            def _():
                loop(BANDS, lambda c: o_up(p, c).start())

            for n in range(PANELS - 1):
                def one(b):
                    @when(p - 1 - n >= 0)
                    def _():
                        pair_r(p - 1 - n, b).wait_recv()
                        pass_e(p - 1 - n, b, True, False)

                    @when(p + 1 + n < PANELS)
                    def _():
                        pair_l(p + 1 + n, b).wait_recv()
                        pass_e(p + 1 + n, b, False, True)

                loop(EARLY // 2, one)
                if n == 0:
                    own_o(0)
                own_o(n + 1)

            def send_rows(k):
                @when(edge)
                def _():
                    def one(g):
                        q = jnp.where(p == 0, k // 2, PANELS - 1 - k // 2)
                        rows_of(q, lax.rem(k, 2), jnp.where(p == 0, CHUNKS - 2 - 2 * g, 2 * g))

                        @when(site < sites - 1)
                        def _():
                            for n in range(2):
                                when(g == n)(rows_next(sent, n, k).start)

                    loop(2, one)

            def hop_and_send(n):
                def half(b):
                    loop(BANDS // 2, lambda c: hop_band(n, b * (BANDS // 2) + c))
                    send_rows(2 * n + 2 + b)

                loop(2, half)

            own_e()
            loop(2, send_rows)
            hop_and_send(0)

            @when(p == 0)
            def _():
                loop(EARLY, lambda i: e_r(0, EARLY + i).start())

            @when(p == 3)
            def _():
                loop(EARLY, lambda i: e_l(3, EARLY - 1 - i).start())

            hop_and_send(1)

            @when(p == 1)
            def _():
                def one(i):
                    j = EARLY + i
                    e_r(1, j).start()
                    e_r(0, j).wait_recv()
                    e_r(0, j).start()

                loop(EARLY, one)

            @when(p == 2)
            def _():
                def one(i):
                    j = EARLY - 1 - i
                    e_l(2, j).start()
                    e_l(3, j).wait_recv()
                    e_l(3, j).start()

                loop(EARLY, one)

            hop_and_send(2)

            @when(p == 1)
            def _():
                def one(i):
                    j = EARLY - 1 - i
                    e_l(1, j).start()
                    e_l(2, j).wait_recv()
                    e_l(2, j).start()
                    e_l(3, j).wait_recv()
                    e_l(3, j).start()

                loop(EARLY, one)

            @when(p == 2)
            def _():
                def one(i):
                    j = EARLY + i
                    e_r(2, j).start()
                    e_r(1, j).wait_recv()
                    e_r(1, j).start()
                    e_r(0, j).wait_recv()
                    e_r(0, j).start()

                loop(EARLY, one)

            @when(edge)
            def _():
                loop(EARLY, lambda i: whole_chunk(EARLY + i))
                loop(EARLY, lambda i: copy_own(nth(i)))

        @when(~edge)
        def _():
            loop(CHUNKS, own_chunk)

        def drain_o(i):
            q, c = i // BANDS, lax.rem(i, BANDS)

            @when(site < sites - 2)
            def _():
                o_up(q, c).wait_send()

            @when((q <= p) & (p < PANELS - 1))
            def _():
                o_r(q, c).wait_send()

            @when((q >= p) & (p > 0))
            def _():
                o_l(q, c).wait_send()

        loop(PANELS * BANDS, drain_o)

        def drain_e(i):
            q, j = i // CHUNKS, lax.rem(i, CHUNKS)

            @when((q <= p) & (p < PANELS - 1))
            def _():
                @when(~odd | (j >= EARLY))
                def _():
                    e_r(q, j).wait_send()

                @when(odd & (q < p) & (j < EARLY // 2))
                def _():
                    pair_r(q, j).wait_send()

            @when((q >= p) & (p > 0))
            def _():
                @when(~odd | (j < EARLY))
                def _():
                    e_l(q, j).wait_send()

                @when(odd & (q > p) & (j >= EARLY) & (j < EARLY + EARLY // 2))
                def _():
                    pair_l(q, j - EARLY).wait_send()

        loop(PANELS * CHUNKS, drain_e)

        def step(i):
            _, j = arrival(i)
            d_over(j).wait_recv()
            columns = pl.ds(pl.multiple_of(j * cols, cols), cols)
            br, bi = drecv[j, 0], drecv[j, 1]
            both = dot(dloc[0], jnp.concatenate([br, bi], axis=1)) + dot(dloc[1], jnp.concatenate([-bi, br], axis=1))
            re, im = both[:, :cols].astype(bf16), both[:, cols:].astype(bf16)
            out_ref[0, :, columns] = re
            out_ref[1, :, columns] = im

        def drain_sent():
            def drain_d(i):
                @when((i < direct_out) & (site < sites - 1) & (~odd | (i >= EARLY)))
                def _():
                    d_next(nth(i)).wait_send()

            loop(CHUNKS, drain_d)

            @when(odd & (site < sites - 1))
            def _():
                for g in range(2):
                    loop(PIECES, lambda k: rows_next(sent, g, k).wait_send())

        when(edge & odd)(drain_sent)

        @when(site == 0)
        def _():
            out_ref[...] = dloc[...]

        def step_pair(i):
            g = pick(i, (0, 1, 3, 2))
            j = jnp.where(low, 2 * g, CHUNKS - 2 - 2 * g)
            loop(2, lambda n: d_over(j + n).wait_recv())
            columns = pl.ds(pl.multiple_of(j * cols, cols), 2 * cols)
            ar, ai = dloc[0], dloc[1]
            br = jnp.concatenate([drecv[j, 0], drecv[j + 1, 0]], axis=1)
            bi = jnp.concatenate([drecv[j, 1], drecv[j + 1, 1]], axis=1)
            out_ref[0, :, columns] = (dot(ar, br) - dot(ai, bi)).astype(bf16)
            out_ref[1, :, columns] = (dot(ar, bi) + dot(ai, br)).astype(bf16)

        @when((site > 0) & ~odd)
        def _():
            loop(CHUNKS // 2, step_pair)

        @when((site > 0) & odd)
        def _():
            loop(CHUNKS, step)

        when(edge & ~odd)(drain_sent)


def shards(forward_props):
    x = forward_props[:, 0]
    _, rows, width = x.shape
    cols = width // CHUNKS
    dma = pltpu.SemaphoreType.DMA
    tm_size = lax.axis_size("tm")
    out = pl.pallas_call(
        functools.partial(kernel, tm_size),
        out_shape=jax.ShapeDtypeStruct(x.shape, bf16),
        in_specs=[pl.BlockSpec(memory_space=pl.ANY)],
        out_specs=pl.BlockSpec(memory_space=pltpu.VMEM),
        scratch_shapes=[
            pltpu.VMEM(x.shape, bf16),
            pltpu.VMEM((2, width, width), bf16),
            pltpu.VMEM((2, width, width), bf16),
            pltpu.VMEM((CHUNKS, 2, width, cols), bf16),
            pltpu.VMEM((CHUNKS, 2, width, cols), bf16),
            pltpu.VMEM((CHUNKS, 2, width, cols), bf16),
            pltpu.VMEM(x.shape, bf16),
            pltpu.VMEM(x.shape, bf16),
            pltpu.VMEM(x.shape, f32),
            dma((CHUNKS + 1,)),
            dma((PANELS, BANDS)),
            dma((PANELS, BANDS)),
            dma((PANELS, BANDS)),
            dma((PANELS, BANDS)),
            dma((PANELS, BANDS)),
            dma((PANELS, CHUNKS)),
            dma((PANELS, CHUNKS)),
            dma((PANELS, CHUNKS)),
            dma((CHUNKS,)),
            dma((CHUNKS,)),
            dma((CHUNKS,)),
            dma((CHUNKS,)),
            pltpu.VMEM(x.shape, bf16),
            dma((BANDS,)),
            dma((BANDS,)),
            dma((2, 2 * PIECES)),
            dma((2, 2 * PIECES)),
            pltpu.VMEM((2, width, 2 * cols), bf16),
        ],
        compiler_params=pltpu.CompilerParams(
            collective_id=0, has_side_effects=True, vmem_limit_bytes=52 * 2**20
        ),
        name="prefix_products",
    )(x)
    return out[:, None]


def solution(mesh):
    placed = (P(None, "tm", "panel", None),)
    return jax.shard_map(
        shards, mesh=mesh, in_specs=placed, out_specs=P(None, "tm", "panel", None), check_vma=False
    )
```
